128 devices in a mesh: row: 8 (over x, y_lo), col: 16 (over z, y_hi, core).
Axes of the slice: x: 4, y: 4 (y_hi: 2, y_lo: 2; y = y_hi * 2 + y_lo), z: 4, core: 2. Of those that a mesh axis runs over, the one named last changes fastest.
Arguments:
- pair: bfloat16 [512, 512, 128], P('row', 'col'), may hold values from -6 to 6
- gain_one: bfloat16 [128], replicated, may hold values from 0.25 to 1.75
- proj_one: bfloat16 [128, 512], replicated, may hold values from -0.5 to 0.5
- bias_one: bfloat16 [128, 4], replicated, may hold values from -6 to 6
- out_one: bfloat16 [128, 128], replicated, may hold values from -0.5 to 0.5
- gain_two: bfloat16 [128], replicated, may hold values from 0.25 to 1.75
- proj_two: bfloat16 [128, 512], replicated, may hold values from -0.5 to 0.5
- bias_two: bfloat16 [128, 4], replicated, may hold values from -6 to 6
- out_two: bfloat16 [128, 128], replicated, may hold values from -0.5 to 0.5
Outputs:
- pair_out: bfloat16 [512, 512, 128], P('row', 'col')
The draws below stay inside these ranges and needn't reach their ends.
All inputs are finite; a program needn't handle non-finite values.
Results may differ from the reference program's by a relative error of at most 0.03.
Values may be sent and summed in bfloat16 or wider, within the bound.
A program may use at most 128 MiB of HBM per device.

```python
import jax
import jax.numpy as jnp
from jax import lax

C = 128
H = 4
DH = 32
N = 512


def draw_bias_one(key, part):
    key = jax.random.fold_in(key, 11)
    return jnp.clip(jax.random.normal(key, (C, H), jnp.float32) * C ** (-0.5), -6.0, 6.0).astype(jnp.bfloat16)


def draw_bias_two(key, part):
    key = jax.random.fold_in(key, 23)
    return jnp.clip(jax.random.normal(key, (C, H), jnp.float32) * C ** (-0.5), -6.0, 6.0).astype(jnp.bfloat16)


def level_of(rng, shape, pieces, smallest, high):
    def one(position, blocks):
        draws = jax.random.uniform(jax.random.fold_in(jax.random.fold_in(rng, 6), position), (blocks,), jnp.float32, smallest / len(pieces), high / len(pieces))
        return jnp.repeat(jnp.exp(draws), shape[position] // blocks).reshape((-1,) + (1,) * (len(shape) - position - 1))

    level = one(*pieces[0])
    for cut in pieces[1:]:
        level = level * one(*cut)
    return level


def noise(key, extent, deviation, limit, split=(), held_as=jnp.bfloat16):
    array = jax.random.normal(key, extent, jnp.float32) * deviation
    if len(split) > 0:
        array = level_of(key, extent, split, -0.22, 0.18) * array
    return jnp.clip(array, min=-limit, max=limit).astype(held_as)


def setup_inputs(seed: int = 0) -> dict:
    key_list = jax.random.split(jax.random.key(seed), 10)
    return {
        "pair": noise(key_list[0], (N, N, C), 1.0, 6.0, ((0, 8), (1, 16))),
        "gain_one": jnp.clip(1.0 + 0.15 * jax.random.normal(key_list[1], (C,), jnp.float32), 0.25, 1.75).astype(jnp.bfloat16),
        "proj_one": noise(key_list[2], (C, 4 * C), C ** -0.5, 0.5),
        "bias_one": draw_bias_one(jax.random.fold_in(key_list[9], 71), 0),
        "out_one": noise(key_list[4], (C, C), C ** -0.5, 0.5),
        "gain_two": jnp.clip(1.0 + 0.15 * jax.random.normal(key_list[5], (C,), jnp.float32), 0.25, 1.75).astype(jnp.bfloat16),
        "proj_two": noise(key_list[6], (C, 4 * C), C ** -0.5, 0.5),
        "bias_two": draw_bias_two(jax.random.fold_in(key_list[9], 71), 0),
        "out_two": noise(key_list[8], (C, C), C ** -0.5, 0.5),
    }


def normalize(pair, gain):
    values = pair.astype(jnp.float32)
    mean = lax.optimization_barrier(jnp.mean(values, axis=-1, keepdims=True))
    spread = lax.optimization_barrier(jnp.mean((values - mean) ** 2, axis=-1, keepdims=True))
    return ((values - mean) * lax.rsqrt(spread + 1e-05) * gain.astype(jnp.float32)).astype(jnp.bfloat16)

def linear(inputs, weight):
    flat = inputs.reshape(-1, inputs.shape[-1])
    result = jnp.dot(flat, weight, preferred_element_type=jnp.float32)
    return result.reshape(inputs.shape[:-1] + (weight.shape[1],))

def attend(query, keys, values, bias):
    score = jnp.einsum('qhd,khd->hqk', query.astype(jnp.float32), keys.astype(jnp.float32)) + bias.astype(jnp.float32)
    prob = jax.nn.softmax(score, axis=-1).astype(jnp.bfloat16)
    return jnp.einsum('hqk,khd->qhd', prob.astype(jnp.float32), values.astype(jnp.float32))

def prepare(pair, gain, proj, bias_weight):
    normed = normalize(pair, gain)
    query = (linear(normed, proj[:, 0:C]) * DH ** (-0.5)).astype(jnp.bfloat16)
    keyval = linear(normed, proj[:, C:3 * C]).astype(jnp.bfloat16)
    gate = jax.nn.sigmoid(linear(normed, proj[:, 3 * C:4 * C]))
    pbias = linear(normed, bias_weight).astype(jnp.bfloat16)
    shape = (N, N, H, DH)
    return (query.reshape(shape), keyval[..., :C].reshape(shape), keyval[..., C:].reshape(shape), gate, pbias)

def reference(pair, gain_one, proj_one, bias_one, out_one, gain_two, proj_two, bias_two, out_two):
    query, keys, values, gate, pbias = prepare(pair, gain_one, proj_one, bias_one)
    start_bias = jnp.transpose(pbias, (2, 0, 1))
    attn = lax.map(lambda group: attend(group[0], group[1], group[2], start_bias), (query, keys, values))
    gated = (gate * attn.reshape(N, N, C)).astype(jnp.bfloat16)
    middle = (pair.astype(jnp.float32) + linear(gated, out_one)).astype(jnp.bfloat16)
    query, keys, values, gate, pbias = prepare(middle, gain_two, proj_two, bias_two)
    end_bias = jnp.transpose(pbias, (2, 1, 0))
    swapped = (jnp.transpose(query, (1, 0, 2, 3)), jnp.transpose(keys, (1, 0, 2, 3)), jnp.transpose(values, (1, 0, 2, 3)))
    attn = lax.map(lambda group: attend(group[0], group[1], group[2], end_bias), swapped)
    attn = jnp.transpose(attn, (1, 0, 2, 3))
    gated = (gate * attn.reshape(N, N, C)).astype(jnp.bfloat16)
    return (middle.astype(jnp.float32) + linear(gated, out_two)).astype(jnp.bfloat16)
```

```python
import jax
import jax.numpy as jnp
from jax import lax
from jax.experimental import pallas as pl
from jax.experimental.pallas import tpu as pltpu
from jax.sharding import PartitionSpec as P

C = 128
H = 4
DH = 32
N = 512
ROWS = 8
COLS = 16
DEVS = ROWS * COLS
OWN = N // DEVS
ROWS_HERE = N // ROWS
COLS_HERE = N // COLS
BLOCKS = 4
LANES = N // BLOCKS
CHUNK = 64
ONES = 16
LOG2E = 1.4426950408889634
MESH = pl.DeviceIdType.MESH
F32 = jnp.float32
BF16 = jnp.bfloat16
VMEM = pl.BlockSpec(memory_space=pltpu.VMEM)


def layer_norm(values, gain):
    mean = jnp.mean(values, axis=-1, keepdims=True)
    centred = values - mean
    spread = jnp.mean(centred * centred, axis=-1, keepdims=True)
    return centred * lax.rsqrt(spread + 1e-05) * gain


def dot(left, right):
    return jnp.dot(left, right, preferred_element_type=F32)


def dot_nt(left, right):
    return lax.dot_general(left, right, (((1,), (1,)), ((), ())), preferred_element_type=F32)


def device_of(x, y, z, core):
    x, y, z, core = lax.rem(x, 4), lax.rem(y, 4), lax.rem(z, 4), lax.rem(core, 2)
    return (x * 2 + lax.rem(y, 2), (z * 2 + y // 2) * 2 + core)


def remote(src, dst, send_sem, recv_sem, target):
    return pltpu.make_async_remote_copy(
        src_ref=src, dst_ref=dst, send_sem=send_sem, recv_sem=recv_sem,
        device_id=target, device_id_type=MESH,
    )


def kernel(
    pair_ref, gain_one_ref, proj_one_ref, bias_one_ref, out_one_ref,
    gain_two_ref, proj_two_ref, bias_two_ref, out_two_ref, block_ref,
    rows, whole_one, whole_two, tiles, columns, result, landed,
    flat_f, chunk_f, small_f, line_f, bias_f, values_f, query, keys, turned, gate_f, prob,
    own_sem, rows_send, rows_recv, plane_send, plane_recv, ring_send, ring_recv, pair_send, pair_recv,
    tile_send, tile_recv, plane2_send, plane2_recv, ring2_send, ring2_recv, pair2_send, pair2_recv,
    back_send, back_recv,
):
    row, col = lax.axis_index("row"), lax.axis_index("col")
    me = row * COLS + col
    x, z, core = row // 2, col // 4, lax.rem(col, 2)
    ylo, yhi = lax.rem(row, 2), lax.rem(col // 2, 2)
    y = 2 * yhi + ylo
    sibling = (row, col + 1 - 2 * core)

    barrier = pltpu.get_barrier_semaphore()

    @pl.loop(1, DEVS)
    def _(step):
        other = lax.rem(me + step, DEVS)
        pl.semaphore_signal(
            barrier, inc=1, device_id=(other // COLS, lax.rem(other, COLS)), device_id_type=MESH
        )

    gain_one = gain_one_ref[...].astype(F32)
    bias_one_t = jnp.transpose(bias_one_ref[...].astype(F32)).astype(BF16)

    @pl.loop(0, 8)
    def _(part):
        values = pair_ref[pl.ds(part * 8, 8)].reshape(256, C).astype(F32)
        flat_f[pl.ds(part * 256, 256), :] = layer_norm(values, gain_one)

    for k in range(16):
        both = jnp.concatenate(
            [flat_f[pl.ds(k, ROWS_HERE, COLS_HERE), :], flat_f[pl.ds(16 + k, ROWS_HERE, COLS_HERE), :]], axis=0
        ).astype(BF16)
        found = dot_nt(bias_one_t, both)
        for head in range(H):
            chunk_f[head * 16 + k, :] = found[head]
    whole_one[x, ylo, z, yhi, core] = chunk_f[...].astype(BF16)

    pl.semaphore_wait(barrier, DEVS - 1)

    def plane_copy(step):
        mine = whole_one.at[x, ylo, z, yhi, core]
        to = device_of(x, y + step // 4, z + lax.rem(step, 4), core)
        return remote(mine, mine, plane_send.at[step], plane_recv.at[step], to)

    def rows_copy(step):
        other = lax.rem(col + step, COLS)
        return remote(
            pair_ref.at[pl.ds(other * OWN, OWN)], rows.at[col], rows_send.at[step], rows_recv.at[step], (row, other)
        )

    def ring_copy(step):
        slab = whole_one.at[x, :, :, :, core]
        return remote(slab, slab, ring_send.at[step], ring_recv.at[step], device_of(x + step, y, z, core))

    def pair_copy(step, plane):
        slab = whole_one.at[plane, :, :, :, core]
        return remote(slab, slab, pair_send.at[step], pair_recv.at[step], sibling)

    @pl.loop(1, 16)
    def _(step):
        plane_copy(step).start()

    @pl.loop(1, COLS)
    def _(step):
        rows_copy(step).start()

    own = pltpu.make_async_copy(pair_ref.at[pl.ds(col * OWN, OWN)], rows.at[col], own_sem)
    own.start()
    proj_one_t = jnp.transpose(proj_one_ref[:, 2 * C :].astype(F32)).astype(BF16)
    proj_two_t = jnp.transpose(proj_two_ref[:, 2 * C :].astype(F32)).astype(BF16)
    bias_two_t = jnp.transpose(bias_two_ref[...].astype(F32)).astype(BF16)
    gain_two = gain_two_ref[...].astype(F32)
    head_of = lax.broadcasted_iota(jnp.int32, (LANES, C), 1) // DH
    for line in range(OWN):
        turned[line, C:, :] = jnp.ones((ONES, N), BF16)

    @pl.loop(1, 16)
    def _(step):
        plane_copy(step).wait_recv()

    for step in (1, 3, 2):
        ring_copy(step).start()
    pair_copy(0, x).start()

    own.wait()

    @pl.loop(1, COLS)
    def _(step):
        rows_copy(step).wait()

    def line_parts(line, values, gain, proj, proj_t):
        normed = layer_norm(values, gain).astype(BF16)
        parts = dot(normed, proj[:, : 2 * C])
        keys[line] = parts[:, C:].astype(BF16)
        for block in range(BLOCKS):
            here = slice(block * LANES, (block + 1) * LANES)
            values_f[line, block] = values[here]
            scaled = parts[here, :C] * (DH ** (-0.5) * LOG2E)
            for head in range(H):
                query[line, block, head * LANES : (head + 1) * LANES, :] = jnp.where(
                    head_of == head, scaled, 0.0
                ).astype(BF16)
        parts_t = dot_nt(proj_t, normed)
        turned[line, :C, :] = parts_t[:C].astype(BF16)
        gate = jax.nn.sigmoid(parts_t[C:])
        for block in range(BLOCKS):
            gate_f[line, block] = gate[:, block * LANES : (block + 1) * LANES]

    def attend(line, block, out):
        for head in range(H):
            here = slice(head * LANES, (head + 1) * LANES)
            score = dot_nt(keys[line], query[line, block, here, :]) + bias_f[head]
            top = jnp.max(score, axis=0, keepdims=True)
            prob[:, here] = jnp.exp2(score - top).astype(BF16)
        summed = dot(turned[line], prob[...])
        attn = jnp.concatenate(
            [
                summed[head * DH : (head + 1) * DH, head * LANES : (head + 1) * LANES]
                / summed[C : C + 1, head * LANES : (head + 1) * LANES]
                for head in range(H)
            ],
            axis=0,
        )
        gated = jnp.transpose(gate_f[line, block] * attn).astype(BF16)
        return values_f[line, block] + dot(gated, out)

    @pl.loop(0, OWN)
    def _(line):
        line_parts(line, rows[:, line].reshape(N, C).astype(F32), gain_one, proj_one_ref, proj_one_t)

    def plane_of(step):
        return lax.rem(x + jnp.where(step == 2, 3, jnp.where(step == 3, 2, step)), 4)

    def tile_copy(group):
        to = (lax.rem(group, ROWS), group // ROWS)
        return remote(tiles.at[group], columns.at[me], tile_send.at[group], tile_recv.at[me], to)

    def plane2_copy(block, step):
        mine = whole_two.at[x, ylo, z, yhi, core, pl.ds(block * 16, 16)]
        to = device_of(x, y + step // 4, z + lax.rem(step, 4), core)
        return remote(mine, mine, plane2_send.at[block, step], plane2_recv.at[block, step], to)

    def ring2_copy(block, step):
        slab = whole_two.at[x, :, :, :, core, pl.ds(block * 16, 16)]
        to = device_of(x + step, y, z, core)
        return remote(slab, slab, ring2_send.at[block, step], ring2_recv.at[block, step], to)

    def pair2_copy(block):
        slab = whole_two.at[:, :, :, :, core, pl.ds(block * 16, 16)]
        return remote(slab, slab, pair2_send.at[block], pair2_recv.at[block], sibling)

    def pass_on(block):
        @pl.loop(1, 16)
        def _(step):
            plane2_copy(block, step).wait_recv()

        for step in (1, 3, 2):
            ring2_copy(block, step).start()

    my_group = col * ROWS + row

    @pl.loop(0, BLOCKS)
    def _(step):
        block = plane_of(step)

        @pl.when(step == 1)
        def _():
            ring_copy(3).wait_recv()
            pair_copy(1, plane_of(1)).start()
            ring_copy(1).wait_recv()
            pair_copy(2, plane_of(2)).start()

        @pl.when(step == 2)
        def _():
            ring_copy(2).wait_recv()
            pair_copy(3, plane_of(3)).start()

        pair_copy(step, block).wait_recv()

        @pl.loop(0, COLS)
        def _(source):
            place = (source // 4, lax.rem(source // 2, 2), lax.rem(source, 2))
            one = whole_one[block, 0, *place].astype(F32) * LOG2E
            two = whole_one[block, 1, *place].astype(F32) * LOG2E
            lower = lax.broadcasted_iota(jnp.int32, (CHUNK, 128), 1) < 64
            left = jnp.where(lower, one, pltpu.roll(two, 64, 1))
            right = jnp.where(lower, pltpu.roll(one, 64, 1), two)
            for head in range(H):
                bias_f[head, pl.ds(source * 32, 16), :] = left[head * 16 : (head + 1) * 16]
                bias_f[head, pl.ds(source * 32 + 16, 16), :] = right[head * 16 : (head + 1) * 16]

        @pl.loop(0, OWN)
        def _(line):
            middle = attend(line, block, out_one_ref[...]).astype(BF16).astype(F32)
            line_f[...] = middle
            for place in range(OWN):
                flat_f[pl.ds(line * OWN + place, 32, 16), :] = line_f[pl.ds(place, 32, OWN), :]
            found = dot_nt(bias_two_t, layer_norm(middle, gain_two).astype(BF16))
            for head in range(H):
                small_f[pl.ds(head * OWN + line, 1), :] = found[head : head + 1]

        whole_two[x, ylo, z, yhi, core, pl.ds(block * 16, 16)] = small_f[...].astype(BF16)
        tiles[pl.ds(block * 32, 32)] = flat_f[:512].astype(BF16).reshape(32, 16, C)

        @pl.loop(1, 16)
        def _(step):
            plane2_copy(block, step).start()

        @pl.loop(0, 32)
        def _(group):
            @pl.when(block * 32 + group != my_group)
            def _():
                tile_copy(block * 32 + group).start()

        @pl.when(step >= 2)
        def _():
            pass_on(plane_of(step - 2))

    pass_on(plane_of(2))
    pass_on(plane_of(3))
    columns[me] = tiles[my_group]

    @pl.loop(0, DEVS)
    def _(source):
        @pl.when(source != me)
        def _():
            remote(
                tiles.at[0], columns.at[source], tile_send.at[0], tile_recv.at[source], sibling
            ).wait_recv()

    flat_f[...] = columns[...].reshape(DEVS * 16, C).astype(F32)

    @pl.loop(0, OWN)
    def _(line):
        line_parts(line, flat_f[pl.ds(line, N, OWN), :], gain_two, proj_two_ref, proj_two_t)

    for delta in (2, 1, 3, 0):
        block = lax.rem(x + delta, 4)
        for step in (1, 3, 2):
            ring2_copy(block, step).wait_recv()
        pair2_copy(block).start()

    def back_copy(other):
        return remote(
            result.at[other], landed.at[row], back_send.at[other], back_recv.at[row], (other, col)
        )

    @pl.loop(0, BLOCKS)
    def _(step):
        block = lax.rem(x + jnp.where(step == 0, 2, jnp.where(step == 2, 3, jnp.where(step == 3, 0, 1))), 4)
        pair2_copy(block).wait_recv()
        flat_f[...] = whole_two[:, :, :, :, :, pl.ds(block * 16, 16)].reshape(DEVS * 16, 128).astype(F32) * LOG2E
        for head in range(H):
            for line in range(OWN):
                bias_f[head, pl.ds(line, DEVS, OWN), :] = flat_f[pl.ds(head * OWN + line, DEVS, 16), :]

        @pl.loop(0, OWN)
        def _(line):
            flat_f[pl.ds(line, LANES, OWN), :] = attend(line, block, out_two_ref[...])

        result[pl.ds(block * 2, 2)] = flat_f[:512].astype(BF16).reshape(2, 256, C)
        for side in range(2):
            @pl.when(block * 2 + side != row)
            def _():
                back_copy(block * 2 + side).start()

    landed[row] = result[row]

    @pl.loop(0, ROWS)
    def _(source):
        @pl.when(source != row)
        def _():
            remote(
                result.at[0], landed.at[source], back_send.at[0], back_recv.at[source], sibling
            ).wait_recv()

    for source in range(ROWS):
        values_f[0, 0] = landed[source, :128].astype(F32)
        values_f[0, 1] = landed[source, 128:].astype(F32)
        for half in range(2):
            for place in range(OWN):
                flat_f[pl.ds(half * 1024 + source * OWN + place, 32, COLS_HERE), :] = values_f[
                    0, half, pl.ds(place, 32, OWN), :
                ]
    block_ref[...] = flat_f[...].astype(BF16).reshape(ROWS_HERE, COLS_HERE, C)

    @pl.loop(1, 16)
    def _(step):
        plane_copy(step).wait_send()

        @pl.loop(0, BLOCKS)
        def _(block):
            plane2_copy(block, step).wait_send()

    for step in range(1, 4):
        ring_copy(step).wait_send()
    for step in range(BLOCKS):
        pair_copy(step, plane_of(step)).wait_send()
        pair2_copy(step).wait_send()
        for delta in range(1, 4):
            ring2_copy(step, delta).wait_send()

    @pl.loop(0, DEVS)
    def _(group):
        @pl.when(group != my_group)
        def _():
            tile_copy(group).wait_send()

    @pl.loop(0, ROWS)
    def _(other):
        @pl.when(other != row)
        def _():
            back_copy(other).wait_send()


def body(pair, gain_one, proj_one, bias_one, out_one, gain_two, proj_two, bias_two, out_two):
    dma = pltpu.SemaphoreType.DMA
    gathered = pltpu.VMEM((4, 2, 4, 2, 2, CHUNK, 128), BF16)
    return pl.pallas_call(
        kernel,
        out_shape=jax.ShapeDtypeStruct((ROWS_HERE, COLS_HERE, C), BF16),
        in_specs=[VMEM] * 9,
        out_specs=VMEM,
        scratch_shapes=[
            pltpu.VMEM((COLS, OWN, COLS_HERE, C), BF16),
            gathered,
            gathered,
            pltpu.VMEM((DEVS, 16, C), BF16),
            pltpu.VMEM((DEVS, 16, C), BF16),
            pltpu.VMEM((ROWS, 256, C), BF16),
            pltpu.VMEM((ROWS, 256, C), BF16),
            pltpu.VMEM((DEVS * 16, C), F32),
            pltpu.VMEM((CHUNK, 128), F32),
            pltpu.VMEM((16, 128), F32),
            pltpu.VMEM((LANES, C), F32),
            pltpu.VMEM((H, N, LANES), F32),
            pltpu.VMEM((OWN, BLOCKS, LANES, C), F32),
            pltpu.VMEM((OWN, BLOCKS, H * LANES, C), BF16),
            pltpu.VMEM((OWN, N, C), BF16),
            pltpu.VMEM((OWN, C + ONES, N), BF16),
            pltpu.VMEM((OWN, BLOCKS, C, LANES), F32),
            pltpu.VMEM((N, H * LANES), BF16),
            dma, dma((COLS,)), dma((COLS,)),
            dma((16,)), dma((16,)), dma((4,)), dma((4,)), dma((4,)), dma((4,)),
            dma((DEVS,)), dma((DEVS,)),
            dma((BLOCKS, 16)), dma((BLOCKS, 16)), dma((BLOCKS, 4)), dma((BLOCKS, 4)),
            dma((BLOCKS,)), dma((BLOCKS,)),
            dma((ROWS,)), dma((ROWS,)),
        ],
        compiler_params=pltpu.CompilerParams(
            collective_id=0, has_side_effects=True, vmem_limit_bytes=48 * 1024 * 1024
        ),
        name="triangle",
    )(pair, gain_one.reshape(1, C), proj_one, bias_one, out_one, gain_two.reshape(1, C), proj_two, bias_two, out_two)


def solution(mesh):
    in_specs = (P("row", "col", None), P(), P(), P(), P(), P(), P(), P(), P())
    out_specs = P("row", "col", None)
    return jax.shard_map(body, mesh=mesh, in_specs=in_specs, out_specs=out_specs, check_vma=False)
```

```python
import jax
import jax.numpy as jnp
from jax import lax
from jax.experimental import pallas as pl
from jax.experimental.pallas import tpu as pltpu
from jax.sharding import PartitionSpec as P

C = 128
H = 4
DH = 32
N = 512
ROWS = 8
COLS = 16
DEVS = ROWS * COLS
OWN = N // DEVS
ROWS_HERE = N // ROWS
COLS_HERE = N // COLS
BLOCKS = 4
LANES = N // BLOCKS
CHUNK = 64
ONES = 16
LOG2E = 1.4426950408889634
MESH = pl.DeviceIdType.MESH
F32 = jnp.float32
BF16 = jnp.bfloat16
VMEM = pl.BlockSpec(memory_space=pltpu.VMEM)


def layer_norm(values, gain):
    mean = jnp.mean(values, axis=-1, keepdims=True)
    centred = values - mean
    spread = jnp.mean(centred * centred, axis=-1, keepdims=True)
    return centred * lax.rsqrt(spread + 1e-05) * gain


def dot(left, right):
    return jnp.dot(left, right, preferred_element_type=F32)


def dot_nt(left, right):
    return lax.dot_general(left, right, (((1,), (1,)), ((), ())), preferred_element_type=F32)


def device_of(x, y, z, core):
    x, y, z, core = lax.rem(x, 4), lax.rem(y, 4), lax.rem(z, 4), lax.rem(core, 2)
    return (x * 2 + lax.rem(y, 2), (z * 2 + y // 2) * 2 + core)


def remote(src, dst, send_sem, recv_sem, target):
    return pltpu.make_async_remote_copy(
        src_ref=src, dst_ref=dst, send_sem=send_sem, recv_sem=recv_sem,
        device_id=target, device_id_type=MESH,
    )


def kernel(
    pair_in, gain_one_in, proj_one_in, bias_one_in, out_one_in,
    gain_two_in, proj_two_in, bias_two_in, out_two_in, landed,
    pair_ref, gain_one_ref, proj_one_ref, bias_one_ref, out_one_ref,
    gain_two_ref, proj_two_ref, bias_two_ref, out_two_ref, in_sem,
    rows, whole_one, whole_two, tiles, columns, result,
    flat_f, chunk_f, small_f, line_f, bias_f, values_f, query, keys, turned, gate_f, prob,
    own_sem, rows_send, rows_recv, plane_send, plane_recv, ring_send, ring_recv, pair_send, pair_recv,
    tile_send, tile_recv, plane2_send, plane2_recv, ring2_send, ring2_recv, pair2_send, pair2_recv,
    back_send, back_recv, joined,
):
    row, col = lax.axis_index("row"), lax.axis_index("col")
    me = row * COLS + col
    x, z, core = row // 2, col // 4, lax.rem(col, 2)
    ylo, yhi = lax.rem(row, 2), lax.rem(col // 2, 2)
    y = 2 * yhi + ylo
    sibling = (row, col + 1 - 2 * core)

    barrier = pltpu.get_barrier_semaphore()

    @pl.loop(1, 32)
    def _(step):
        other = device_of(x, y + step // 8, z + lax.rem(step // 2, 4), core + lax.rem(step, 2))
        pl.semaphore_signal(barrier, inc=1, device_id=other, device_id_type=MESH)

    for step in range(1, 4):
        pl.semaphore_signal(barrier, inc=1, device_id=device_of(x + step, y, z, core), device_id_type=MESH)

    sources = (
        pair_in, bias_one_in, gain_one_in, proj_one_in, out_one_in, gain_two_in, bias_two_in, proj_two_in, out_two_in
    )
    places = (
        pair_ref, bias_one_ref, gain_one_ref, proj_one_ref, out_one_ref, gain_two_ref, bias_two_ref, proj_two_ref,
        out_two_ref,
    )
    fetches = [
        pltpu.make_async_copy(source, place, in_sem.at[index])
        for index, (source, place) in enumerate(zip(sources, places))
    ]
    for fetch in fetches:
        fetch.start()
    for fetch in fetches[:3]:
        fetch.wait()

    gain_one = gain_one_ref[...].astype(F32)
    bias_one_t = bias_one_ref[...]

    @pl.loop(0, 8)
    def _(part):
        values = pair_ref[pl.ds(part * 8, 8)].reshape(256, C).astype(F32)
        flat_f[pl.ds(part * 256, 256), :] = layer_norm(values, gain_one)

    for k in range(16):
        both = jnp.concatenate(
            [flat_f[pl.ds(k, ROWS_HERE, COLS_HERE), :], flat_f[pl.ds(16 + k, ROWS_HERE, COLS_HERE), :]], axis=0
        ).astype(BF16)
        found = dot_nt(bias_one_t, both)
        for head in range(H):
            chunk_f[head * 16 + k, :] = found[head]
    whole_one[x, ylo, z, yhi, core] = chunk_f[...].astype(BF16)

    pl.semaphore_wait(barrier, 34)
    for step in range(1, 4):
        pl.semaphore_signal(joined, inc=1, device_id=device_of(x + step, y, z, core), device_id_type=MESH)

    def plane_copy(step):
        mine = whole_one.at[x, ylo, z, yhi, core]
        to = device_of(x, y + step // 4, z + lax.rem(step, 4), core)
        return remote(mine, mine, plane_send.at[step], plane_recv.at[step], to)

    def rows_copy(step):
        other = lax.rem(col + step, COLS)
        return remote(
            pair_ref.at[pl.ds(other * OWN, OWN)], rows.at[col], rows_send.at[step], rows_recv.at[step], (row, other)
        )

    def ring_copy(step):
        slab = whole_one.at[x, :, :, :, core]
        return remote(slab, slab, ring_send.at[step], ring_recv.at[step], device_of(x + step, y, z, core))

    def pair_copy(step, plane):
        slab = whole_one.at[plane, :, :, :, core]
        return remote(slab, slab, pair_send.at[step], pair_recv.at[step], sibling)

    @pl.loop(1, 16)
    def _(step):
        plane_copy(step).start()

    @pl.loop(1, COLS)
    def _(step):
        rows_copy(step).start()

    own = pltpu.make_async_copy(pair_ref.at[pl.ds(col * OWN, OWN)], rows.at[col], own_sem)
    own.start()
    for fetch in fetches[3:]:
        fetch.wait()
    proj_one_t = jnp.transpose(proj_one_ref[:, 2 * C :].astype(F32)).astype(BF16)
    proj_two_t = jnp.transpose(proj_two_ref[:, 2 * C :].astype(F32)).astype(BF16)
    bias_two_t = bias_two_ref[...]
    gain_two = gain_two_ref[...].astype(F32)
    head_of = lax.broadcasted_iota(jnp.int32, (LANES, C), 1) // DH
    for line in range(OWN):
        turned[line, C:, :] = jnp.ones((ONES, N), BF16)

    @pl.loop(1, 16)
    def _(step):
        plane_copy(step).wait_recv()

    for step in (1, 3, 2):
        ring_copy(step).start()
    pair_copy(0, x).start()

    own.wait()

    @pl.loop(1, COLS)
    def _(step):
        rows_copy(step).wait()

    def line_parts(line, values, gain, proj, proj_t):
        normed = layer_norm(values, gain).astype(BF16)
        parts = dot(normed, proj[:, : 2 * C])
        keys[line] = parts[:, C:].astype(BF16)
        for block in range(BLOCKS):
            here = slice(block * LANES, (block + 1) * LANES)
            values_f[line, block] = values[here]
            scaled = parts[here, :C] * (DH ** (-0.5) * LOG2E)
            for head in range(H):
                query[line, block, head * LANES : (head + 1) * LANES, :] = jnp.where(
                    head_of == head, scaled, 0.0
                ).astype(BF16)
        parts_t = dot_nt(proj_t, normed)
        turned[line, :C, :] = parts_t[:C].astype(BF16)
        gate = jax.nn.sigmoid(parts_t[C:])
        for block in range(BLOCKS):
            gate_f[line, block] = gate[:, block * LANES : (block + 1) * LANES]

    def attend(block, out):
        for line in range(OWN):
            for pair in range(H // 2):
                both = dot_nt(keys[line], query[line, block, pair * 2 * LANES : (pair + 1) * 2 * LANES, :])
                for side in range(2):
                    head = pair * 2 + side
                    score = both[:, side * LANES : (side + 1) * LANES] + bias_f[head]
                    top = jnp.max(score, axis=0, keepdims=True)
                    prob[line, :, head * LANES : (head + 1) * LANES] = jnp.exp2(score - top).astype(BF16)
        gated = []
        for line in range(OWN):
            summed = dot(turned[line], prob[line])
            attn = jnp.concatenate(
                [
                    summed[head * DH : (head + 1) * DH, head * LANES : (head + 1) * LANES]
                    / summed[C : C + 1, head * LANES : (head + 1) * LANES]
                    for head in range(H)
                ],
                axis=0,
            )
            gated.append(jnp.transpose(gate_f[line, block] * attn).astype(BF16))
        update = dot(jnp.concatenate(gated, axis=0), out)
        return jnp.concatenate([values_f[line, block] for line in range(OWN)], axis=0) + update

    @pl.loop(0, OWN)
    def _(line):
        line_parts(line, rows[:, line].reshape(N, C).astype(F32), gain_one, proj_one_ref, proj_one_t)

    def plane_of(step):
        return lax.rem(x + jnp.where(step == 2, 3, jnp.where(step == 3, 2, step)), 4)

    def tile_copy(group):
        to = (lax.rem(group, ROWS), group // ROWS)
        return remote(tiles.at[group], columns.at[me], tile_send.at[group], tile_recv.at[me], to)

    def plane2_copy(block, step):
        mine = whole_two.at[x, ylo, z, yhi, core, pl.ds(block * 16, 16)]
        to = device_of(x, y + step // 4, z + lax.rem(step, 4), core)
        return remote(mine, mine, plane2_send.at[block, step], plane2_recv.at[block, step], to)

    def ring2_copy(block, step):
        slab = whole_two.at[x, :, :, :, core, pl.ds(block * 16, 16)]
        to = device_of(x + step, y, z, core)
        return remote(slab, slab, ring2_send.at[block, step], ring2_recv.at[block, step], to)

    def pair2_copy(block):
        slab = whole_two.at[:, :, :, :, core, pl.ds(block * 16, 16)]
        return remote(slab, slab, pair2_send.at[block], pair2_recv.at[block], sibling)

    def pass_on(block):
        @pl.loop(1, 16)
        def _(step):
            plane2_copy(block, step).wait_recv()

        for step in (1, 3, 2):
            ring2_copy(block, step).start()

    my_group = col * ROWS + row

    @pl.loop(0, BLOCKS)
    def _(step):
        block = plane_of(step)

        @pl.when(step == 1)
        def _():
            ring_copy(3).wait_recv()
            pair_copy(1, plane_of(1)).start()
            ring_copy(1).wait_recv()
            pair_copy(2, plane_of(2)).start()

        @pl.when(step == 2)
        def _():
            ring_copy(2).wait_recv()
            pair_copy(3, plane_of(3)).start()

        pair_copy(step, block).wait_recv()

        @pl.loop(0, 4)
        def _(depth):
            lower = lax.broadcasted_iota(jnp.int32, (CHUNK, 128), 1) < 64
            for part in range(4):
                one = whole_one[block, 0, depth, part // 2, part % 2].astype(F32) * LOG2E
                two = whole_one[block, 1, depth, part // 2, part % 2].astype(F32) * LOG2E
                left = jnp.where(lower, one, pltpu.roll(two, 64, 1))
                right = jnp.where(lower, pltpu.roll(one, 64, 1), two)
                first = depth * 128 + part * 32
                for head in range(H):
                    bias_f[head, pl.ds(first, 16), :] = left[head * 16 : (head + 1) * 16]
                    bias_f[head, pl.ds(first + 16, 16), :] = right[head * 16 : (head + 1) * 16]

        middle = attend(block, out_one_ref[...]).astype(BF16).astype(F32)
        line_f[...] = middle
        for line in range(OWN):
            for place in range(OWN):
                flat_f[pl.ds(line * OWN + place, 32, 16), :] = line_f[pl.ds(line * LANES + place, 32, OWN), :]
        found = dot_nt(bias_two_t, layer_norm(middle, gain_two).astype(BF16))
        for line in range(OWN):
            for head in range(H):
                small_f[head * OWN + line, :] = found[head, line * LANES : (line + 1) * LANES]
        whole_two[x, ylo, z, yhi, core, pl.ds(block * 16, 16)] = small_f[...].astype(BF16)
        tiles[pl.ds(block * 32, 32)] = flat_f[:512].astype(BF16).reshape(32, 16, C)

        @pl.when(step == 0)
        def _():
            pl.semaphore_wait(joined, 3)

        @pl.loop(1, 16)
        def _(step):
            plane2_copy(block, step).start()

        @pl.loop(0, 32)
        def _(group):
            @pl.when(block * 32 + group != my_group)
            def _():
                tile_copy(block * 32 + group).start()

        @pl.when(step >= 2)
        def _():
            pass_on(plane_of(step - 2))

    pass_on(plane_of(2))
    pass_on(plane_of(3))
    columns[me] = tiles[my_group]

    @pl.loop(0, DEVS)
    def _(source):
        @pl.when(source != me)
        def _():
            remote(
                tiles.at[0], columns.at[source], tile_send.at[0], tile_recv.at[source], sibling
            ).wait_recv()

    flat_f[...] = columns[...].reshape(DEVS * 16, C).astype(F32)

    for line in range(OWN):
        line_parts(line, flat_f[pl.ds(line, N, OWN), :], gain_two, proj_two_ref, proj_two_t)

    for delta in (2, 1, 3, 0):
        block = lax.rem(x + delta, 4)
        for step in (1, 3, 2):
            ring2_copy(block, step).wait_recv()
        pair2_copy(block).start()

    def back_copy(other):
        return remote(
            result.at[other], landed.at[row], back_send.at[other], back_recv.at[row], (other, col)
        )

    @pl.loop(0, BLOCKS)
    def _(step):
        block = lax.rem(x + jnp.where(step == 0, 2, jnp.where(step == 2, 3, jnp.where(step == 3, 0, 1))), 4)
        pair2_copy(block).wait_recv()
        flat_f[...] = whole_two[:, :, :, :, :, pl.ds(block * 16, 16)].reshape(DEVS * 16, 128).astype(F32) * LOG2E
        for head in range(H):
            for line in range(OWN):
                bias_f[head, pl.ds(line, DEVS, OWN), :] = flat_f[pl.ds(head * OWN + line, DEVS, 16), :]

        found = attend(block, out_two_ref[...])
        for line in range(OWN):
            flat_f[pl.ds(line, LANES, OWN), :] = found[line * LANES : (line + 1) * LANES]
        result[pl.ds(block * 2, 2)] = flat_f[:512].astype(BF16).reshape(2, 256, C)
        for side in range(2):
            @pl.when(block * 2 + side != row)
            def _():
                back_copy(block * 2 + side).start()

    own_result = pltpu.make_async_copy(result.at[row], landed.at[row], own_sem)
    own_result.start()
    own_result.wait()

    @pl.loop(0, ROWS)
    def _(source):
        @pl.when(source != row)
        def _():
            remote(
                result.at[0], landed.at[source], back_send.at[0], back_recv.at[source], sibling
            ).wait_recv()

    @pl.loop(1, 16)
    def _(step):
        plane_copy(step).wait_send()

        @pl.loop(0, BLOCKS)
        def _(block):
            plane2_copy(block, step).wait_send()

    for step in range(1, 4):
        ring_copy(step).wait_send()
    for step in range(BLOCKS):
        pair_copy(step, plane_of(step)).wait_send()
        pair2_copy(step).wait_send()
        for delta in range(1, 4):
            ring2_copy(step, delta).wait_send()

    @pl.loop(0, DEVS)
    def _(group):
        @pl.when(group != my_group)
        def _():
            tile_copy(group).wait_send()

    @pl.loop(0, ROWS)
    def _(other):
        @pl.when(other != row)
        def _():
            back_copy(other).wait_send()


def arrange(landed_ref, block_ref, flat_f, block_f):
    for source in range(ROWS):
        flat_f[...] = landed_ref[source].astype(F32)
        for place in range(OWN):
            block_f[pl.ds(source * OWN + place, 16, COLS_HERE), :] = flat_f[pl.ds(place, 16, OWN), :]
    block_ref[...] = block_f[...].astype(BF16).reshape(16, COLS_HERE, C)


def body(pair, gain_one, proj_one, bias_one, out_one, gain_two, proj_two, bias_two, out_two):
    dma = pltpu.SemaphoreType.DMA
    gathered = pltpu.VMEM((4, 2, 4, 2, 2, CHUNK, 128), BF16)
    landed = pl.pallas_call(
        kernel,
        out_shape=jax.ShapeDtypeStruct((ROWS, 256, C), BF16),
        in_specs=[pl.BlockSpec(memory_space=pltpu.HBM)] * 9,
        out_specs=pl.BlockSpec(memory_space=pl.ANY),
        scratch_shapes=[
            pltpu.VMEM((ROWS_HERE, COLS_HERE, C), BF16),
            pltpu.VMEM((1, C), BF16),
            pltpu.VMEM((C, 4 * C), BF16),
            pltpu.VMEM((H, C), BF16),
            pltpu.VMEM((C, C), BF16),
            pltpu.VMEM((1, C), BF16),
            pltpu.VMEM((C, 4 * C), BF16),
            pltpu.VMEM((H, C), BF16),
            pltpu.VMEM((C, C), BF16),
            dma((9,)),
            pltpu.VMEM((COLS, OWN, COLS_HERE, C), BF16),
            gathered,
            gathered,
            pltpu.VMEM((DEVS, 16, C), BF16),
            pltpu.VMEM((DEVS, 16, C), BF16),
            pltpu.VMEM((ROWS, 256, C), BF16),
            pltpu.VMEM((DEVS * 16, C), F32),
            pltpu.VMEM((CHUNK, 128), F32),
            pltpu.VMEM((16, 128), F32),
            pltpu.VMEM((OWN * LANES, C), F32),
            pltpu.VMEM((H, N, LANES), F32),
            pltpu.VMEM((OWN, BLOCKS, LANES, C), F32),
            pltpu.VMEM((OWN, BLOCKS, H * LANES, C), BF16),
            pltpu.VMEM((OWN, N, C), BF16),
            pltpu.VMEM((OWN, C + ONES, N), BF16),
            pltpu.VMEM((OWN, BLOCKS, C, LANES), F32),
            pltpu.VMEM((OWN, N, H * LANES), BF16),
            dma, dma((COLS,)), dma((COLS,)),
            dma((16,)), dma((16,)), dma((4,)), dma((4,)), dma((4,)), dma((4,)),
            dma((DEVS,)), dma((DEVS,)),
            dma((BLOCKS, 16)), dma((BLOCKS, 16)), dma((BLOCKS, 4)), dma((BLOCKS, 4)),
            dma((BLOCKS,)), dma((BLOCKS,)),
            dma((ROWS,)), dma((ROWS,)), pltpu.SemaphoreType.REGULAR,
        ],
        compiler_params=pltpu.CompilerParams(
            collective_id=0, has_side_effects=True, vmem_limit_bytes=60 * 1024 * 1024
        ),
        name="triangle",
    )(
        pair, gain_one.reshape(1, C), proj_one, bias_one.T, out_one,
        gain_two.reshape(1, C), proj_two, bias_two.T, out_two,
    )
    return landed.reshape(ROWS, ROWS_HERE, OWN, C).transpose(1, 0, 2, 3).reshape(ROWS_HERE, COLS_HERE, C)


def solution(mesh):
    in_specs = (P("row", "col", None), P(), P(), P(), P(), P(), P(), P(), P())
    out_specs = P("row", "col", None)
    return jax.shard_map(body, mesh=mesh, in_specs=in_specs, out_specs=out_specs, check_vma=False)
```

```python
import jax
import jax.numpy as jnp
from jax import lax
from jax.experimental import pallas as pl
from jax.experimental.pallas import tpu as pltpu
from jax.sharding import PartitionSpec as P

C = 128
H = 4
DH = 32
N = 512
ROWS = 8
COLS = 16
DEVS = ROWS * COLS
OWN = N // DEVS
ROWS_HERE = N // ROWS
COLS_HERE = N // COLS
BLOCKS = 4
LANES = N // BLOCKS
CHUNK = 64
ONES = 16
LOG2E = 1.4426950408889634
MESH = pl.DeviceIdType.MESH
F32 = jnp.float32
BF16 = jnp.bfloat16
VMEM = pl.BlockSpec(memory_space=pltpu.VMEM)


def layer_norm(values, gain):
    mean = jnp.mean(values, axis=-1, keepdims=True)
    centred = values - mean
    spread = jnp.mean(centred * centred, axis=-1, keepdims=True)
    return centred * lax.rsqrt(spread + 1e-05) * gain


def dot(left, right):
    return jnp.dot(left, right, preferred_element_type=F32)


def dot_nt(left, right):
    return lax.dot_general(left, right, (((1,), (1,)), ((), ())), preferred_element_type=F32)


def device_of(x, y, z, core):
    x, y, z, core = lax.rem(x, 4), lax.rem(y, 4), lax.rem(z, 4), lax.rem(core, 2)
    return (x * 2 + lax.rem(y, 2), (z * 2 + y // 2) * 2 + core)


def remote(src, dst, send_sem, recv_sem, target):
    return pltpu.make_async_remote_copy(
        src_ref=src, dst_ref=dst, send_sem=send_sem, recv_sem=recv_sem,
        device_id=target, device_id_type=MESH,
    )


def kernel(
    pair_in, gain_one_in, proj_one_in, bias_one_in, out_one_in,
    gain_two_in, proj_two_in, bias_two_in, out_two_in, landed,
    pair_ref, gain_one_ref, proj_one_ref, bias_one_ref, out_one_ref,
    gain_two_ref, proj_two_ref, bias_two_ref, out_two_ref, in_sem,
    rows, whole_one, whole_two, tiles, columns, result,
    flat_f, chunk_f, small_f, line_f, bias_f, values_f, query, keys, turned, gate_f, prob,
    own_sem, rows_send, rows_recv, plane_send, plane_recv, ring_send, ring_recv, pair_send, pair_recv,
    tile_send, tile_recv, plane2_send, plane2_recv, ring2_send, ring2_recv, pair2_send, pair2_recv,
    back_send, back_recv, joined,
):
    row, col = lax.axis_index("row"), lax.axis_index("col")
    me = row * COLS + col
    x, z, core = row // 2, col // 4, lax.rem(col, 2)
    ylo, yhi = lax.rem(row, 2), lax.rem(col // 2, 2)
    y = 2 * yhi + ylo
    sibling = (row, col + 1 - 2 * core)

    barrier = pltpu.get_barrier_semaphore()

    @pl.loop(1, 32)
    def _(step):
        other = device_of(x, y + step // 8, z + lax.rem(step // 2, 4), core + lax.rem(step, 2))
        pl.semaphore_signal(barrier, inc=1, device_id=other, device_id_type=MESH)

    for step in range(1, 4):
        pl.semaphore_signal(barrier, inc=1, device_id=device_of(x + step, y, z, core), device_id_type=MESH)

    sources = (
        pair_in, bias_one_in, gain_one_in, proj_one_in, out_one_in, gain_two_in, bias_two_in, proj_two_in, out_two_in
    )
    places = (
        pair_ref, bias_one_ref, gain_one_ref, proj_one_ref, out_one_ref, gain_two_ref, bias_two_ref, proj_two_ref,
        out_two_ref,
    )
    fetches = [
        pltpu.make_async_copy(source, place, in_sem.at[index])
        for index, (source, place) in enumerate(zip(sources, places))
    ]
    for fetch in fetches:
        fetch.start()
    for fetch in fetches[:3]:
        fetch.wait()

    gain_one = gain_one_ref[...].astype(F32)
    bias_one_t = bias_one_ref[...]

    @pl.loop(0, 8)
    def _(part):
        values = pair_ref[pl.ds(part * 8, 8)].reshape(256, C).astype(F32)
        flat_f[pl.ds(part * 256, 256), :] = layer_norm(values, gain_one)

    for k in range(16):
        both = jnp.concatenate(
            [flat_f[pl.ds(k, ROWS_HERE, COLS_HERE), :], flat_f[pl.ds(16 + k, ROWS_HERE, COLS_HERE), :]], axis=0
        ).astype(BF16)
        found = dot_nt(bias_one_t, both)
        for head in range(H):
            chunk_f[head * 16 + k, :] = found[head]
    whole_one[x, ylo, z, yhi, core] = chunk_f[...].astype(BF16)

    pl.semaphore_wait(barrier, 34)
    for step in range(1, 4):
        pl.semaphore_signal(joined, inc=1, device_id=device_of(x + step, y, z, core), device_id_type=MESH)

    def many(count, send_sem, recv_sem):
        some = pl.ds(0, count)
        return remote(tiles.at[some], columns.at[some], send_sem, recv_sem, sibling)

    def plane_copy(step):
        mine = whole_one.at[x, ylo, z, yhi, core]
        to = device_of(x, y + step // 4, z + lax.rem(step, 4), core)
        return remote(mine, mine, plane_send, plane_recv, to)

    def rows_copy(step):
        other = lax.rem(col + step, COLS)
        return remote(
            pair_ref.at[pl.ds(other * OWN, OWN)], rows.at[col], rows_send, rows_recv, (row, other)
        )

    def ring_copy(step):
        slab = whole_one.at[x, :, :, :, core]
        return remote(slab, slab, ring_send.at[step], ring_recv.at[step], device_of(x + step, y, z, core))

    def pair_copy(step, plane):
        slab = whole_one.at[plane, :, :, :, core]
        return remote(slab, slab, pair_send.at[step], pair_recv.at[step], sibling)

    @pl.loop(1, 16)
    def _(step):
        plane_copy(step).start()

    @pl.loop(1, COLS)
    def _(step):
        rows_copy(step).start()

    own = pltpu.make_async_copy(pair_ref.at[pl.ds(col * OWN, OWN)], rows.at[col], own_sem)
    own.start()
    for fetch in fetches[3:]:
        fetch.wait()
    proj_one_t = jnp.transpose(proj_one_ref[:, 2 * C :].astype(F32)).astype(BF16)
    proj_two_t = jnp.transpose(proj_two_ref[:, 2 * C :].astype(F32)).astype(BF16)
    bias_two_t = bias_two_ref[...]
    gain_two = gain_two_ref[...].astype(F32)
    head_of = lax.broadcasted_iota(jnp.int32, (LANES, C), 1) // DH
    for line in range(OWN):
        turned[line, C:, :] = jnp.ones((ONES, N), BF16)

    many(60, plane_send, plane_recv).wait_recv()

    for step in (1, 3, 2):
        ring_copy(step).start()
    pair_copy(0, x).start()

    own.wait()

    many(120, rows_send, rows_recv).wait()

    def line_parts(line, values, gain, proj, proj_t):
        normed = layer_norm(values, gain).astype(BF16)
        parts = dot(normed, proj[:, : 2 * C])
        keys[line] = parts[:, C:].astype(BF16)
        for block in range(BLOCKS):
            here = slice(block * LANES, (block + 1) * LANES)
            values_f[line, block] = values[here]
            scaled = parts[here, :C] * (DH ** (-0.5) * LOG2E)
            for head in range(H):
                query[line, block, head * LANES : (head + 1) * LANES, :] = jnp.where(
                    head_of == head, scaled, 0.0
                ).astype(BF16)
        parts_t = dot_nt(proj_t, normed)
        turned[line, :C, :] = parts_t[:C].astype(BF16)
        gate = jax.nn.sigmoid(parts_t[C:])
        for block in range(BLOCKS):
            gate_f[line, block] = gate[:, block * LANES : (block + 1) * LANES]

    def attend(block, out):
        for line in range(OWN):
            for pair in range(H // 2):
                both = dot_nt(keys[line], query[line, block, pair * 2 * LANES : (pair + 1) * 2 * LANES, :])
                for side in range(2):
                    head = pair * 2 + side
                    score = both[:, side * LANES : (side + 1) * LANES] + bias_f[head]
                    top = jnp.max(score, axis=0, keepdims=True)
                    prob[line, :, head * LANES : (head + 1) * LANES] = jnp.exp2(score - top).astype(BF16)
        gated = []
        for line in range(OWN):
            summed = dot(turned[line], prob[line])
            attn = jnp.concatenate(
                [
                    summed[head * DH : (head + 1) * DH, head * LANES : (head + 1) * LANES]
                    / summed[C : C + 1, head * LANES : (head + 1) * LANES]
                    for head in range(H)
                ],
                axis=0,
            )
            gated.append(jnp.transpose(gate_f[line, block] * attn).astype(BF16))
        update = dot(jnp.concatenate(gated, axis=0), out)
        return jnp.concatenate([values_f[line, block] for line in range(OWN)], axis=0) + update

    for line in range(OWN):
        line_parts(line, rows[:, line].reshape(N, C).astype(F32), gain_one, proj_one_ref, proj_one_t)

    def plane_of(step):
        return lax.rem(x + jnp.where(step == 2, 3, jnp.where(step == 3, 2, step)), 4)

    def tile_copy(group):
        to = (lax.rem(group, ROWS), group // ROWS)
        return remote(tiles.at[group], columns.at[me], tile_send, tile_recv, to)

    def all_tiles():
        return many(DEVS - 1, tile_send, tile_recv)

    def plane2_copy(block, step):
        mine = whole_two.at[x, ylo, z, yhi, core, pl.ds(block * 16, 16)]
        to = device_of(x, y + step // 4, z + lax.rem(step, 4), core)
        return remote(mine, mine, plane2_send.at[block], plane2_recv.at[block], to)

    def ring2_copy(block, step):
        slab = whole_two.at[x, :, :, :, core, pl.ds(block * 16, 16)]
        to = device_of(x + step, y, z, core)
        return remote(slab, slab, ring2_send.at[block], ring2_recv.at[block], to)

    def pair2_copy(block):
        slab = whole_two.at[:, :, :, :, core, pl.ds(block * 16, 16)]
        return remote(slab, slab, pair2_send.at[block], pair2_recv.at[block], sibling)

    def pass_on(block):
        many(15, plane2_send.at[block], plane2_recv.at[block]).wait_recv()
        for step in (1, 3, 2):
            ring2_copy(block, step).start()

    my_group = col * ROWS + row

    @pl.loop(0, BLOCKS)
    def _(step):
        block = plane_of(step)

        @pl.when(step == 1)
        def _():
            ring_copy(3).wait_recv()
            pair_copy(1, plane_of(1)).start()
            ring_copy(1).wait_recv()
            pair_copy(2, plane_of(2)).start()

        @pl.when(step == 2)
        def _():
            ring_copy(2).wait_recv()
            pair_copy(3, plane_of(3)).start()

        pair_copy(step, block).wait_recv()

        @pl.loop(0, 4)
        def _(depth):
            lower = lax.broadcasted_iota(jnp.int32, (CHUNK, 128), 1) < 64
            for part in range(4):
                one = whole_one[block, 0, depth, part // 2, part % 2].astype(F32) * LOG2E
                two = whole_one[block, 1, depth, part // 2, part % 2].astype(F32) * LOG2E
                left = jnp.where(lower, one, pltpu.roll(two, 64, 1))
                right = jnp.where(lower, pltpu.roll(one, 64, 1), two)
                first = depth * 128 + part * 32
                for head in range(H):
                    bias_f[head, pl.ds(first, 16), :] = left[head * 16 : (head + 1) * 16]
                    bias_f[head, pl.ds(first + 16, 16), :] = right[head * 16 : (head + 1) * 16]

        middle = attend(block, out_one_ref[...]).astype(BF16).astype(F32)
        found = dot_nt(bias_two_t, layer_norm(middle, gain_two).astype(BF16))
        for line in range(OWN):
            for head in range(H):
                small_f[head * OWN + line, :] = found[head, line * LANES : (line + 1) * LANES]
        whole_two[x, ylo, z, yhi, core, pl.ds(block * 16, 16)] = small_f[...].astype(BF16)

        @pl.when(step == 0)
        def _():
            pl.semaphore_wait(joined, 3)

        @pl.loop(1, 16)
        def _(step):
            plane2_copy(block, step).start()

        line_f[...] = middle
        for line in range(OWN):
            for place in range(OWN):
                flat_f[pl.ds(line * OWN + place, 32, 16), :] = line_f[pl.ds(line * LANES + place, 32, OWN), :]
        tiles[pl.ds(block * 32, 32)] = flat_f[:512].astype(BF16).reshape(32, 16, C)

        @pl.loop(0, 32)
        def _(group):
            @pl.when(block * 32 + group != my_group)
            def _():
                tile_copy(block * 32 + group).start()

        @pl.when(step >= 2)
        def _():
            pass_on(plane_of(step - 2))

    pass_on(plane_of(2))
    pass_on(plane_of(3))
    columns[me] = tiles[my_group]

    all_tiles().wait_recv()
    flat_f[...] = columns[...].reshape(DEVS * 16, C).astype(F32)

    def to_other_core(delta):
        block = lax.rem(x + delta, 4)
        many(48, ring2_send.at[block], ring2_recv.at[block]).wait_recv()
        pair2_copy(block).start()

    for line in range(OWN):
        line_parts(line, flat_f[pl.ds(line, N, OWN), :], gain_two, proj_two_ref, proj_two_t)
        if line == 1:
            to_other_core(2)
    for delta in (1, 3, 0):
        to_other_core(delta)

    def back_copy(other):
        return remote(
            result.at[other], landed.at[row], back_send, back_recv, (other, col)
        )

    @pl.loop(0, BLOCKS)
    def _(step):
        block = lax.rem(x + jnp.where(step == 0, 2, jnp.where(step == 2, 3, jnp.where(step == 3, 0, 1))), 4)
        pair2_copy(block).wait_recv()
        flat_f[...] = whole_two[:, :, :, :, :, pl.ds(block * 16, 16)].reshape(DEVS * 16, 128).astype(F32) * LOG2E
        for head in range(H):
            for line in range(OWN):
                bias_f[head, pl.ds(line, DEVS, OWN), :] = flat_f[pl.ds(head * OWN + line, DEVS, 16), :]

        found = attend(block, out_two_ref[...])
        for line in range(OWN):
            flat_f[pl.ds(line, LANES, OWN), :] = found[line * LANES : (line + 1) * LANES]
        result[pl.ds(block * 2, 2)] = flat_f[:512].astype(BF16).reshape(2, 256, C)
        for side in range(2):
            @pl.when(block * 2 + side != row)
            def _():
                back_copy(block * 2 + side).start()

    own_result = pltpu.make_async_copy(result.at[row], landed.at[row], own_sem)
    own_result.start()
    own_result.wait()

    many(60, plane_send, plane_recv).wait_send()
    for step in range(1, 4):
        ring_copy(step).wait_send()
    for step in range(BLOCKS):
        pair_copy(step, plane_of(step)).wait_send()
        many(64, pair2_send.at[step], pair2_recv.at[step]).wait_send()
        many(15, plane2_send.at[step], plane2_recv.at[step]).wait_send()
        many(48, ring2_send.at[step], ring2_recv.at[step]).wait_send()
    all_tiles().wait_send()

    all_back = many(7 * 16, back_send, back_recv)
    all_back.wait_recv()
    all_back.wait_send()


def arrange(landed_ref, block_ref, flat_f, block_f):
    for source in range(ROWS):
        flat_f[...] = landed_ref[source].astype(F32)
        for place in range(OWN):
            block_f[pl.ds(source * OWN + place, 16, COLS_HERE), :] = flat_f[pl.ds(place, 16, OWN), :]
    block_ref[...] = block_f[...].astype(BF16).reshape(16, COLS_HERE, C)


def body(pair, gain_one, proj_one, bias_one, out_one, gain_two, proj_two, bias_two, out_two):
    dma = pltpu.SemaphoreType.DMA
    gathered = pltpu.VMEM((4, 2, 4, 2, 2, CHUNK, 128), BF16)
    landed = pl.pallas_call(
        kernel,
        out_shape=jax.ShapeDtypeStruct((ROWS, 256, C), BF16),
        in_specs=[pl.BlockSpec(memory_space=pltpu.HBM)] * 9,
        out_specs=pl.BlockSpec(memory_space=pl.ANY),
        scratch_shapes=[
            pltpu.VMEM((ROWS_HERE, COLS_HERE, C), BF16),
            pltpu.VMEM((1, C), BF16),
            pltpu.VMEM((C, 4 * C), BF16),
            pltpu.VMEM((H, C), BF16),
            pltpu.VMEM((C, C), BF16),
            pltpu.VMEM((1, C), BF16),
            pltpu.VMEM((C, 4 * C), BF16),
            pltpu.VMEM((H, C), BF16),
            pltpu.VMEM((C, C), BF16),
            dma((9,)),
            pltpu.VMEM((COLS, OWN, COLS_HERE, C), BF16),
            gathered,
            gathered,
            pltpu.VMEM((DEVS, 16, C), BF16),
            pltpu.VMEM((DEVS, 16, C), BF16),
            pltpu.VMEM((ROWS, 256, C), BF16),
            pltpu.VMEM((DEVS * 16, C), F32),
            pltpu.VMEM((CHUNK, 128), F32),
            pltpu.VMEM((16, 128), F32),
            pltpu.VMEM((OWN * LANES, C), F32),
            pltpu.VMEM((H, N, LANES), F32),
            pltpu.VMEM((OWN, BLOCKS, LANES, C), F32),
            pltpu.VMEM((OWN, BLOCKS, H * LANES, C), BF16),
            pltpu.VMEM((OWN, N, C), BF16),
            pltpu.VMEM((OWN, C + ONES, N), BF16),
            pltpu.VMEM((OWN, BLOCKS, C, LANES), F32),
            pltpu.VMEM((OWN, N, H * LANES), BF16),
            dma, dma, dma,
            dma, dma, dma((4,)), dma((4,)), dma((4,)), dma((4,)),
            dma, dma,
            dma((BLOCKS,)), dma((BLOCKS,)), dma((BLOCKS,)), dma((BLOCKS,)), dma((BLOCKS,)), dma((BLOCKS,)),
            dma, dma, pltpu.SemaphoreType.REGULAR,
        ],
        compiler_params=pltpu.CompilerParams(
            collective_id=0, has_side_effects=True, vmem_limit_bytes=60 * 1024 * 1024
        ),
        name="triangle",
    )(
        pair, gain_one.reshape(1, C), proj_one, bias_one.T, out_one,
        gain_two.reshape(1, C), proj_two, bias_two.T, out_two,
    )
    return landed.reshape(ROWS, ROWS_HERE, OWN, C).transpose(1, 0, 2, 3).reshape(ROWS_HERE, COLS_HERE, C)


def solution(mesh):
    in_specs = (P("row", "col", None), P(), P(), P(), P(), P(), P(), P(), P())
    out_specs = P("row", "col", None)
    return jax.shard_map(body, mesh=mesh, in_specs=in_specs, out_specs=out_specs, check_vma=False)
```

```python
import jax
import jax.numpy as jnp
from jax import lax
from jax.experimental import pallas as pl
from jax.experimental.pallas import tpu as pltpu
from jax.sharding import PartitionSpec as P

C = 128
H = 4
DH = 32
N = 512
ROWS = 8
COLS = 16
DEVS = ROWS * COLS
OWN = N // DEVS
ROWS_HERE = N // ROWS
COLS_HERE = N // COLS
BLOCKS = 4
LANES = N // BLOCKS
CHUNK = 64
ONES = 16
LOG2E = 1.4426950408889634
MESH = pl.DeviceIdType.MESH
FAR_FIRST = sorted(range(1, 16), key=lambda step: -min(step // 4, 4 - step // 4) - min(step % 4, 4 - step % 4))
F32 = jnp.float32
BF16 = jnp.bfloat16
VMEM = pl.BlockSpec(memory_space=pltpu.VMEM)


def layer_norm(values, gain):
    mean = jnp.mean(values, axis=-1, keepdims=True)
    centred = values - mean
    spread = jnp.mean(centred * centred, axis=-1, keepdims=True)
    return centred * lax.rsqrt(spread + 1e-05) * gain


def dot(left, right):
    return jnp.dot(left, right, preferred_element_type=F32)


def dot_nt(left, right):
    return lax.dot_general(left, right, (((1,), (1,)), ((), ())), preferred_element_type=F32)


def device_of(x, y, z, core):
    x, y, z, core = lax.rem(x, 4), lax.rem(y, 4), lax.rem(z, 4), lax.rem(core, 2)
    return (x * 2 + lax.rem(y, 2), (z * 2 + y // 2) * 2 + core)


def remote(src, dst, send_sem, recv_sem, target):
    return pltpu.make_async_remote_copy(
        src_ref=src, dst_ref=dst, send_sem=send_sem, recv_sem=recv_sem,
        device_id=target, device_id_type=MESH,
    )


def kernel(
    pair_in, gain_one_in, proj_one_in, bias_one_in, out_one_in,
    gain_two_in, proj_two_in, bias_two_in, out_two_in, landed,
    pair_ref, gain_one_ref, proj_one_ref, bias_one_ref, out_one_ref,
    gain_two_ref, proj_two_ref, bias_two_ref, out_two_ref, in_sem,
    rows, whole_one, whole_two, tiles, columns, result,
    flat_f, chunk_f, small_f, line_f, bias_f, values_f, query, keys, turned, gate_f, prob,
    own_sem, rows_send, rows_recv, plane_send, plane_recv, ring_send, ring_recv, pair_send, pair_recv,
    tile_send, tile_recv, plane2_send, plane2_recv, ring2_send, ring2_recv, pair2_send, pair2_recv,
    back_send, back_recv, joined,
):
    row, col = lax.axis_index("row"), lax.axis_index("col")
    me = row * COLS + col
    x, z, core = row // 2, col // 4, lax.rem(col, 2)
    ylo, yhi = lax.rem(row, 2), lax.rem(col // 2, 2)
    y = 2 * yhi + ylo
    sibling = (row, col + 1 - 2 * core)

    barrier = pltpu.get_barrier_semaphore()
    sources = (
        pair_in, bias_one_in, gain_one_in, proj_one_in, out_one_in, gain_two_in, bias_two_in, proj_two_in, out_two_in
    )
    places = (
        pair_ref, bias_one_ref, gain_one_ref, proj_one_ref, out_one_ref, gain_two_ref, bias_two_ref, proj_two_ref,
        out_two_ref,
    )
    fetches = [
        pltpu.make_async_copy(source, place, in_sem.at[index])
        for index, (source, place) in enumerate(zip(sources, places))
    ]
    for fetch in fetches:
        fetch.start()

    @pl.loop(1, 32)
    def _(step):
        other = device_of(x, y + step // 8, z + lax.rem(step // 2, 4), core + lax.rem(step, 2))
        pl.semaphore_signal(barrier, inc=1, device_id=other, device_id_type=MESH)

    for step in range(1, 4):
        pl.semaphore_signal(barrier, inc=1, device_id=device_of(x + step, y, z, core), device_id_type=MESH)

    for fetch in fetches[:3]:
        fetch.wait()

    gain_one = gain_one_ref[...].astype(F32)
    bias_one_t = bias_one_ref[...]

    @pl.loop(0, 8)
    def _(part):
        values = pair_ref[pl.ds(part * 8, 8)].reshape(256, C).astype(F32)
        flat_f[pl.ds(part * 256, 256), :] = layer_norm(values, gain_one)

    for k in range(16):
        both = jnp.concatenate(
            [flat_f[pl.ds(k, ROWS_HERE, COLS_HERE), :], flat_f[pl.ds(16 + k, ROWS_HERE, COLS_HERE), :]], axis=0
        ).astype(BF16)
        found = dot_nt(bias_one_t, both)
        for head in range(H):
            chunk_f[head * 16 + k, :] = found[head]
    whole_one[x, ylo, z, yhi, core] = chunk_f[...].astype(BF16)

    pl.semaphore_wait(barrier, 34)
    for step in range(1, 4):
        pl.semaphore_signal(joined, inc=1, device_id=device_of(x + step, y, z, core), device_id_type=MESH)

    def many(count, send_sem, recv_sem):
        some = pl.ds(0, count)
        return remote(tiles.at[some], columns.at[some], send_sem, recv_sem, sibling)

    def plane_copy(step):
        mine = whole_one.at[x, ylo, z, yhi, core]
        to = device_of(x, y + step // 4, z + lax.rem(step, 4), core)
        return remote(mine, mine, plane_send, plane_recv, to)

    def rows_copy(step):
        other = lax.rem(col + step, COLS)
        return remote(
            pair_ref.at[pl.ds(other * OWN, OWN)], rows.at[col], rows_send, rows_recv, (row, other)
        )

    def ring_copy(step):
        slab = whole_one.at[x, :, :, :, core]
        return remote(slab, slab, ring_send.at[step], ring_recv.at[step], device_of(x + step, y, z, core))

    def onward_copy(step):
        half = pl.ds(0, CHUNK // 2) if step == 1 else pl.ds(CHUNK // 2, CHUNK // 2)
        slab = whole_one.at[lax.rem(x + 4 - step, 4), :, :, :, core, half]
        to = device_of(x + step, y, z, core)
        return remote(slab, slab, ring_send.at[step - 1], ring_recv.at[step - 1], to)

    def pair_copy(step, plane):
        slab = whole_one.at[plane, :, :, :, core]
        return remote(slab, slab, pair_send.at[step], pair_recv.at[step], sibling)

    for step in FAR_FIRST:
        plane_copy(step).start()

    for step in sorted(range(1, COLS), key=lambda step: -min(step // 4, 4 - step // 4)):
        rows_copy(step).start()

    own = pltpu.make_async_copy(pair_ref.at[pl.ds(col * OWN, OWN)], rows.at[col], own_sem)
    own.start()
    for fetch in fetches[3:]:
        fetch.wait()
    proj_one_t = jnp.transpose(proj_one_ref[:, 2 * C :].astype(F32)).astype(BF16)
    proj_two_t = jnp.transpose(proj_two_ref[:, 2 * C :].astype(F32)).astype(BF16)
    bias_two_t = bias_two_ref[...]
    gain_two = gain_two_ref[...].astype(F32)
    head_of = lax.broadcasted_iota(jnp.int32, (LANES, C), 1) // DH
    for line in range(OWN):
        turned[line, C:, :] = jnp.ones((ONES, N), BF16)

    many(60, plane_send, plane_recv).wait_recv()

    for step in (1, 3):
        ring_copy(step).start()
    pair_copy(0, x).start()

    own.wait()

    many(120, rows_send, rows_recv).wait()

    def line_parts(line, values, gain, proj, proj_t):
        normed = layer_norm(values, gain).astype(BF16)
        parts = dot(normed, proj[:, : 2 * C])
        keys[line] = parts[:, C:].astype(BF16)
        for block in range(BLOCKS):
            here = slice(block * LANES, (block + 1) * LANES)
            values_f[line, block] = values[here]
            scaled = parts[here, :C] * (DH ** (-0.5) * LOG2E)
            for head in range(H):
                query[line, block, head * LANES : (head + 1) * LANES, :] = jnp.where(
                    head_of == head, scaled, 0.0
                ).astype(BF16)
        parts_t = dot_nt(proj_t, normed)
        turned[line, :C, :] = parts_t[:C].astype(BF16)
        gate = jax.nn.sigmoid(parts_t[C:])
        for block in range(BLOCKS):
            gate_f[line, block] = gate[:, block * LANES : (block + 1) * LANES]

    def attend(block, out, between):
        for line in range(OWN):
            for pair in range(H // 2):
                both = dot_nt(keys[line], query[line, block, pair * 2 * LANES : (pair + 1) * 2 * LANES, :])
                for side in range(2):
                    head = pair * 2 + side
                    score = both[:, side * LANES : (side + 1) * LANES] + bias_f[head]
                    top = jnp.max(score, axis=0, keepdims=True)
                    prob[line, :, head * LANES : (head + 1) * LANES] = jnp.exp2(score - top).astype(BF16)
        between()
        gated = []
        for line in range(OWN):
            attn = []
            for head in range(H):
                lhs = jnp.concatenate([turned[line, head * DH : (head + 1) * DH, :], turned[line, C:, :]], axis=0)
                summed = dot(lhs, prob[line, :, head * LANES : (head + 1) * LANES])
                attn.append(summed[:DH] * (1.0 / summed[DH : DH + 1]))
            attn = jnp.concatenate(attn, axis=0)
            gated.append(jnp.transpose(gate_f[line, block] * attn).astype(BF16))
        update = dot(jnp.concatenate(gated, axis=0), out)
        return jnp.concatenate([values_f[line, block] for line in range(OWN)], axis=0) + update

    for line in range(OWN):
        line_parts(line, rows[:, line].reshape(N, C).astype(F32), gain_one, proj_one_ref, proj_one_t)

    def plane_of(step):
        return lax.rem(x + jnp.where(step == 2, 3, jnp.where(step == 3, 2, step)), 4)

    def tile_copy(group):
        to = (lax.rem(group, ROWS), group // ROWS)
        return remote(tiles.at[group], columns.at[me], tile_send, tile_recv, to)

    def all_tiles():
        return many(DEVS - 1, tile_send, tile_recv)

    def at_step(step):
        return pl.ds(step * 16, 16)

    def plane2_copy(axis, step, index):
        mine = whole_two.at[x, ylo, z, yhi, core, at_step(step)]
        one, two = index // 4, index % 4
        to = device_of(x + one, y, z + two, core) if axis == "y" else device_of(x + one, y + two, z, core)
        return remote(mine, mine, plane2_send.at[step], plane2_recv.at[step], to)

    def ring2_copy(axis, step, index):
        if axis == "y":
            slab, to = whole_two.at[:, ylo, :, yhi, core, at_step(step)], device_of(x, y + index, z, core)
        else:
            slab, to = whole_two.at[:, :, z, :, core, at_step(step)], device_of(x, y, z + index, core)
        return remote(slab, slab, ring2_send.at[step], ring2_recv.at[step], to)

    def pair2_copy(step):
        slab = whole_two.at[:, :, :, :, core, at_step(step)]
        return remote(slab, slab, pair2_send.at[step], pair2_recv.at[step], sibling)

    def pass_on(axis, step):
        many(15, plane2_send.at[step], plane2_recv.at[step]).wait_recv()
        for index in (1, 3, 2):
            ring2_copy(axis, step, index).start()

    def to_other_core(step):
        many(48, ring2_send.at[step], ring2_recv.at[step]).wait_recv()
        pair2_copy(step).start()

    my_group = col * ROWS + row

    @pl.loop(0, BLOCKS)
    def _(step):
        block = plane_of(step)

        pair_copy(step, block).wait_recv()

        @pl.loop(0, 4)
        def _(depth):
            lower = lax.broadcasted_iota(jnp.int32, (CHUNK, 128), 1) < 64
            for part in range(4):
                one = whole_one[block, 0, depth, part // 2, part % 2].astype(F32) * LOG2E
                two = whole_one[block, 1, depth, part // 2, part % 2].astype(F32) * LOG2E
                left = jnp.where(lower, one, pltpu.roll(two, 64, 1))
                right = jnp.where(lower, pltpu.roll(one, 64, 1), two)
                first = depth * 128 + part * 32
                for head in range(H):
                    bias_f[head, pl.ds(first, 16), :] = left[head * 16 : (head + 1) * 16]
                    bias_f[head, pl.ds(first + 16, 16), :] = right[head * 16 : (head + 1) * 16]

        def fetch_next():
            @pl.when(step == 0)
            def _():
                ring_copy(3).wait_recv()
                onward_copy(3).start()
                pair_copy(1, plane_of(1)).start()
                ring_copy(1).wait_recv()
                onward_copy(1).start()
                pair_copy(2, plane_of(2)).start()

            @pl.when(step == 1)
            def _():
                onward_copy(1).wait_recv()
                onward_copy(3).wait_recv()
                pair_copy(3, plane_of(3)).start()

        middle = attend(block, out_one_ref[...], fetch_next).astype(BF16).astype(F32)
        found = dot_nt(bias_two_t, layer_norm(middle, gain_two).astype(BF16))
        for line in range(OWN):
            for head in range(H):
                small_f[head * OWN + line, :] = found[head, line * LANES : (line + 1) * LANES]
        whole_two[x, ylo, z, yhi, core, at_step(step)] = small_f[...].astype(BF16)

        @pl.when(step == 0)
        def _():
            pl.semaphore_wait(joined, 3)

        for parity, axis in enumerate("yz"):
            @pl.when(lax.rem(step, 2) == parity)
            def _():
                for index in FAR_FIRST:
                    plane2_copy(axis, step, index).start()

        line_f[...] = middle
        for line in range(OWN):
            for place in range(OWN):
                flat_f[pl.ds(line * OWN + place, 32, 16), :] = line_f[pl.ds(line * LANES + place, 32, OWN), :]
        tiles[pl.ds(block * 32, 32)] = flat_f[:512].astype(BF16).reshape(32, 16, C)

        @pl.loop(0, 32, unroll=8)
        def _(index):
            group = block * 32 + lax.rem(index + me, 32)

            @pl.when(group != my_group)
            def _():
                tile_copy(group).start()

        for late, axis in ((2, "y"), (3, "z")):
            @pl.when(step == late)
            def _():
                pass_on(axis, late - 2)

    pass_on("y", 2)
    to_other_core(0)
    pass_on("z", 3)
    to_other_core(1)
    columns[me] = tiles[my_group]

    all_tiles().wait_recv()
    flat_f[...] = columns[...].reshape(DEVS * 16, C).astype(F32)

    for line in range(OWN):
        line_parts(line, flat_f[pl.ds(line, N, OWN), :], gain_two, proj_two_ref, proj_two_t)
    for step in (2, 3):
        to_other_core(step)
    for step in range(BLOCKS):
        pair2_copy(step).wait_recv()

    def back_copy(other):
        return remote(
            result.at[other], landed.at[row], back_send, back_recv, (other, col)
        )

    @pl.loop(0, BLOCKS)
    def _(step):
        block = lax.rem(x + jnp.where(step == 0, 2, jnp.where(step == 2, 3, jnp.where(step == 3, 0, 1))), 4)
        for plane in range(4):
            delta = lax.rem(block - plane + 4, 4)
            made = jnp.where(delta == 2, 3, jnp.where(delta == 3, 2, delta))
            flat_f[plane * 512 : (plane + 1) * 512, :] = (
                whole_two[plane, :, :, :, :, at_step(made)].reshape(512, 128).astype(F32) * LOG2E
            )
        for head in range(H):
            for line in range(OWN):
                bias_f[head, pl.ds(line, DEVS, OWN), :] = flat_f[pl.ds(head * OWN + line, DEVS, 16), :]

        found = attend(block, out_two_ref[...], lambda: None)
        for line in range(OWN):
            flat_f[pl.ds(line, LANES, OWN), :] = found[line * LANES : (line + 1) * LANES]
        result[pl.ds(block * 2, 2)] = flat_f[:512].astype(BF16).reshape(2, 256, C)
        for side in range(2):
            @pl.when(block * 2 + side != row)
            def _():
                back_copy(block * 2 + side).start()

    own_result = pltpu.make_async_copy(result.at[row], landed.at[row], own_sem)
    own_result.start()
    own_result.wait()

    many(60, plane_send, plane_recv).wait_send()
    for step in (1, 3):
        ring_copy(step).wait_send()
        onward_copy(step).wait_send()
    for step in range(BLOCKS):
        pair_copy(step, plane_of(step)).wait_send()
        many(64, pair2_send.at[step], pair2_recv.at[step]).wait_send()
        many(15, plane2_send.at[step], plane2_recv.at[step]).wait_send()
        many(48, ring2_send.at[step], ring2_recv.at[step]).wait_send()
    all_tiles().wait_send()

    all_back = many(7 * 16, back_send, back_recv)
    all_back.wait_recv()
    all_back.wait_send()


def arrange(landed_ref, block_ref, flat_f, block_f):
    for source in range(ROWS):
        flat_f[...] = landed_ref[source].astype(F32)
        for place in range(OWN):
            block_f[pl.ds(source * OWN + place, 16, COLS_HERE), :] = flat_f[pl.ds(place, 16, OWN), :]
    block_ref[...] = block_f[...].astype(BF16).reshape(16, COLS_HERE, C)


def body(pair, gain_one, proj_one, bias_one, out_one, gain_two, proj_two, bias_two, out_two):
    dma = pltpu.SemaphoreType.DMA
    gathered = pltpu.VMEM((4, 2, 4, 2, 2, CHUNK, 128), BF16)
    landed = pl.pallas_call(
        kernel,
        out_shape=jax.ShapeDtypeStruct((ROWS, 256, C), BF16),
        in_specs=[pl.BlockSpec(memory_space=pltpu.HBM)] * 9,
        out_specs=pl.BlockSpec(memory_space=pl.ANY),
        scratch_shapes=[
            pltpu.VMEM((ROWS_HERE, COLS_HERE, C), BF16),
            pltpu.VMEM((1, C), BF16),
            pltpu.VMEM((C, 4 * C), BF16),
            pltpu.VMEM((H, C), BF16),
            pltpu.VMEM((C, C), BF16),
            pltpu.VMEM((1, C), BF16),
            pltpu.VMEM((C, 4 * C), BF16),
            pltpu.VMEM((H, C), BF16),
            pltpu.VMEM((C, C), BF16),
            dma((9,)),
            pltpu.VMEM((COLS, OWN, COLS_HERE, C), BF16),
            gathered,
            gathered,
            pltpu.VMEM((DEVS, 16, C), BF16),
            pltpu.VMEM((DEVS, 16, C), BF16),
            pltpu.VMEM((ROWS, 256, C), BF16),
            pltpu.VMEM((DEVS * 16, C), F32),
            pltpu.VMEM((CHUNK, 128), F32),
            pltpu.VMEM((16, 128), F32),
            pltpu.VMEM((OWN * LANES, C), F32),
            pltpu.VMEM((H, N, LANES), F32),
            pltpu.VMEM((OWN, BLOCKS, LANES, C), F32),
            pltpu.VMEM((OWN, BLOCKS, H * LANES, C), BF16),
            pltpu.VMEM((OWN, N, C), BF16),
            pltpu.VMEM((OWN, C + ONES, N), BF16),
            pltpu.VMEM((OWN, BLOCKS, C, LANES), F32),
            pltpu.VMEM((OWN, N, H * LANES), BF16),
            dma, dma, dma,
            dma, dma, dma((4,)), dma((4,)), dma((4,)), dma((4,)),
            dma, dma,
            dma((BLOCKS,)), dma((BLOCKS,)), dma((BLOCKS,)), dma((BLOCKS,)), dma((BLOCKS,)), dma((BLOCKS,)),
            dma, dma, pltpu.SemaphoreType.REGULAR,
        ],
        compiler_params=pltpu.CompilerParams(
            collective_id=0, has_side_effects=True, vmem_limit_bytes=60 * 1024 * 1024
        ),
        name="triangle",
    )(
        pair, gain_one.reshape(1, C), proj_one, bias_one.T, out_one,
        gain_two.reshape(1, C), proj_two, bias_two.T, out_two,
    )
    return landed.reshape(ROWS, ROWS_HERE, OWN, C).transpose(1, 0, 2, 3).reshape(ROWS_HERE, COLS_HERE, C)


def solution(mesh):
    in_specs = (P("row", "col", None), P(), P(), P(), P(), P(), P(), P(), P())
    out_specs = P("row", "col", None)
    return jax.shard_map(body, mesh=mesh, in_specs=in_specs, out_specs=out_specs, check_vma=False)
```

```python
import jax
import jax.numpy as jnp
from jax import lax
from jax.experimental import pallas as pl
from jax.experimental.pallas import tpu as pltpu
from jax.sharding import PartitionSpec as P

C = 128
H = 4
DH = 32
N = 512
ROWS = 8
COLS = 16
DEVS = ROWS * COLS
OWN = N // DEVS
ROWS_HERE = N // ROWS
COLS_HERE = N // COLS
BLOCKS = 4
LANES = N // BLOCKS
CHUNK = 64
ONES = 16
LOG2E = 1.4426950408889634
MESH = pl.DeviceIdType.MESH
FAR_FIRST = sorted(range(1, 16), key=lambda step: -min(step // 4, 4 - step // 4) - min(step % 4, 4 - step % 4))
F32 = jnp.float32
BF16 = jnp.bfloat16
VMEM = pl.BlockSpec(memory_space=pltpu.VMEM)


def layer_norm(values, gain):
    mean = jnp.mean(values, axis=-1, keepdims=True)
    centred = values - mean
    spread = jnp.mean(centred * centred, axis=-1, keepdims=True)
    return centred * lax.rsqrt(spread + 1e-05) * gain


def dot(left, right):
    return jnp.dot(left, right, preferred_element_type=F32)


def dot_nt(left, right):
    return lax.dot_general(left, right, (((1,), (1,)), ((), ())), preferred_element_type=F32)


def device_of(x, y, z, core):
    x, y, z, core = lax.rem(x, 4), lax.rem(y, 4), lax.rem(z, 4), lax.rem(core, 2)
    return (x * 2 + lax.rem(y, 2), (z * 2 + y // 2) * 2 + core)


def remote(src, dst, send_sem, recv_sem, target):
    return pltpu.make_async_remote_copy(
        src_ref=src, dst_ref=dst, send_sem=send_sem, recv_sem=recv_sem,
        device_id=target, device_id_type=MESH,
    )


def kernel(
    pair_in, gain_one_in, proj_one_in, bias_one_in, out_one_in,
    gain_two_in, proj_two_in, bias_two_in, out_two_in, landed,
    pair_ref, gain_one_ref, proj_one_ref, bias_one_ref, out_one_ref,
    gain_two_ref, proj_two_ref, bias_two_ref, out_two_ref, in_sem,
    rows, whole_one, whole_two, tiles, columns, result,
    flat_f, chunk_f, small_f, line_f, bias_f, values_f, query, keys, turned, gate_f, prob,
    own_sem, rows_send, rows_recv, plane_send, plane_recv, ring_send, ring_recv, pair_send, pair_recv,
    tile_send, tile_recv, plane2_send, plane2_recv, ring2_send, ring2_recv, pair2_send, pair2_recv,
    back_send, back_recv, joined,
):
    row, col = lax.axis_index("row"), lax.axis_index("col")
    me = row * COLS + col
    x, z, core = row // 2, col // 4, lax.rem(col, 2)
    ylo, yhi = lax.rem(row, 2), lax.rem(col // 2, 2)
    y = 2 * yhi + ylo
    sibling = (row, col + 1 - 2 * core)

    barrier = pltpu.get_barrier_semaphore()
    sources = (
        pair_in, bias_one_in, gain_one_in, proj_one_in, out_one_in, gain_two_in, bias_two_in, proj_two_in, out_two_in
    )
    places = (
        pair_ref, bias_one_ref, gain_one_ref, proj_one_ref, out_one_ref, gain_two_ref, bias_two_ref, proj_two_ref,
        out_two_ref,
    )
    fetches = [
        pltpu.make_async_copy(source, place, in_sem.at[index])
        for index, (source, place) in enumerate(zip(sources, places))
    ]
    for fetch in fetches:
        fetch.start()

    @pl.loop(1, 32)
    def _(step):
        other = device_of(x, y + step // 8, z + lax.rem(step // 2, 4), core + lax.rem(step, 2))
        pl.semaphore_signal(barrier, inc=1, device_id=other, device_id_type=MESH)

    for step in range(1, 4):
        pl.semaphore_signal(barrier, inc=1, device_id=device_of(x + step, y, z, core), device_id_type=MESH)

    for fetch in fetches[:3]:
        fetch.wait()

    gain_one = gain_one_ref[...].astype(F32)
    bias_one_t = bias_one_ref[...]

    @pl.loop(0, 8)
    def _(part):
        values = pair_ref[pl.ds(part * 8, 8)].reshape(256, C).astype(F32)
        flat_f[pl.ds(part * 256, 256), :] = layer_norm(values, gain_one)

    for k in range(16):
        both = jnp.concatenate(
            [flat_f[pl.ds(k, ROWS_HERE, COLS_HERE), :], flat_f[pl.ds(16 + k, ROWS_HERE, COLS_HERE), :]], axis=0
        ).astype(BF16)
        found = dot_nt(bias_one_t, both)
        for head in range(H):
            chunk_f[head * 16 + k, :] = found[head]
    whole_one[x, ylo, z, yhi, core] = chunk_f[...].astype(BF16)

    pl.semaphore_wait(barrier, 34)
    for step in range(1, 4):
        pl.semaphore_signal(joined, inc=1, device_id=device_of(x + step, y, z, core), device_id_type=MESH)

    def many(count, send_sem, recv_sem):
        some = pl.ds(0, count)
        return remote(tiles.at[some], columns.at[some], send_sem, recv_sem, sibling)

    def plane_copy(step):
        mine = whole_one.at[x, ylo, z, yhi, core]
        to = device_of(x, y + step // 4, z + lax.rem(step, 4), core)
        return remote(mine, mine, plane_send, plane_recv, to)

    def rows_copy(step):
        other = lax.rem(col + step, COLS)
        return remote(
            pair_ref.at[pl.ds(other * OWN, OWN)], rows.at[col], rows_send, rows_recv, (row, other)
        )

    def ring_copy(step):
        slab = whole_one.at[x, :, :, :, core]
        return remote(slab, slab, ring_send.at[step], ring_recv.at[step], device_of(x + step, y, z, core))

    def onward_copy(step):
        half = pl.ds(0, CHUNK // 2) if step == 1 else pl.ds(CHUNK // 2, CHUNK // 2)
        slab = whole_one.at[lax.rem(x + 4 - step, 4), :, :, :, core, half]
        to = device_of(x + step, y, z, core)
        return remote(slab, slab, ring_send.at[step - 1], ring_recv.at[step - 1], to)

    def pair_copy(step, plane):
        slab = whole_one.at[plane, :, :, :, core]
        return remote(slab, slab, pair_send.at[step], pair_recv.at[step], sibling)

    for step in FAR_FIRST:
        plane_copy(step).start()

    for step in sorted(range(1, COLS), key=lambda step: -min(step // 4, 4 - step // 4)):
        rows_copy(step).start()

    own = pltpu.make_async_copy(pair_ref.at[pl.ds(col * OWN, OWN)], rows.at[col], own_sem)
    own.start()
    for fetch in fetches[3:]:
        fetch.wait()
    proj_one_t = jnp.transpose(proj_one_ref[:, 2 * C :].astype(F32)).astype(BF16)
    proj_two_t = jnp.transpose(proj_two_ref[:, 2 * C :].astype(F32)).astype(BF16)
    bias_two_t = bias_two_ref[...]
    gain_two = gain_two_ref[...].astype(F32)
    head_of = lax.broadcasted_iota(jnp.int32, (LANES, C), 1) // DH
    for line in range(OWN):
        turned[line, C:, :] = jnp.ones((ONES, N), BF16)

    many(60, plane_send, plane_recv).wait_recv()

    for step in (1, 3):
        ring_copy(step).start()
    pair_copy(0, x).start()

    own.wait()

    many(120, rows_send, rows_recv).wait()

    def line_parts(line, values, gain, proj, proj_t):
        normed = layer_norm(values, gain).astype(BF16)
        parts = dot(normed, proj[:, : 2 * C])
        keys[line] = parts[:, C:].astype(BF16)
        for block in range(BLOCKS):
            here = slice(block * LANES, (block + 1) * LANES)
            values_f[line, block] = values[here]
            scaled = parts[here, :C] * (DH ** (-0.5) * LOG2E)
            for head in range(H):
                query[line, block, head * LANES : (head + 1) * LANES, :] = jnp.where(
                    head_of == head, scaled, 0.0
                ).astype(BF16)
        parts_t = dot_nt(proj_t, normed)
        turned[line, :C, :] = parts_t[:C].astype(BF16)
        gate = jax.nn.sigmoid(parts_t[C:])
        for block in range(BLOCKS):
            gate_f[line, block] = gate[:, block * LANES : (block + 1) * LANES]

    def attend(block, out, between):
        for line in range(OWN):
            for pair in range(H // 2):
                both = dot_nt(keys[line], query[line, block, pair * 2 * LANES : (pair + 1) * 2 * LANES, :])
                for side in range(2):
                    head = pair * 2 + side
                    score = both[:, side * LANES : (side + 1) * LANES] + bias_f[head]
                    top = jnp.max(score, axis=0, keepdims=True)
                    prob[line, :, head * LANES : (head + 1) * LANES] = jnp.exp2(score - top).astype(BF16)
        between()
        gated = []
        for line in range(OWN):
            attn = []
            for head in range(H):
                lhs = jnp.concatenate([turned[line, head * DH : (head + 1) * DH, :], turned[line, C:, :]], axis=0)
                summed = dot(lhs, prob[line, :, head * LANES : (head + 1) * LANES])
                attn.append(summed[:DH] * (1.0 / summed[DH : DH + 1]))
            attn = jnp.concatenate(attn, axis=0)
            gated.append(jnp.transpose(gate_f[line, block] * attn).astype(BF16))
        update = dot(jnp.concatenate(gated, axis=0), out)
        return jnp.concatenate([values_f[line, block] for line in range(OWN)], axis=0) + update

    for line in range(OWN):
        line_parts(line, rows[:, line].reshape(N, C).astype(F32), gain_one, proj_one_ref, proj_one_t)

    def plane_of(step):
        return lax.rem(x + jnp.where(step == 2, 3, jnp.where(step == 3, 2, step)), 4)

    def tile_copy(group):
        to = (lax.rem(group, ROWS), group // ROWS)
        return remote(tiles.at[group], columns.at[me], tile_send, tile_recv, to)

    def all_tiles():
        return many(DEVS - 1, tile_send, tile_recv)

    def at_step(step):
        return pl.ds(step * 16, 16)

    def plane2_copy(axis, step, index):
        mine = whole_two.at[x, ylo, z, yhi, core, at_step(step)]
        one, two = index // 4, index % 4
        to = device_of(x + one, y, z + two, core) if axis == "y" else device_of(x + one, y + two, z, core)
        return remote(mine, mine, plane2_send.at[step], plane2_recv.at[step], to)

    def ring2_copy(axis, step, index):
        if axis == "y":
            slab, to = whole_two.at[:, ylo, :, yhi, core, at_step(step)], device_of(x, y + index, z, core)
        else:
            slab, to = whole_two.at[:, :, z, :, core, at_step(step)], device_of(x, y, z + index, core)
        return remote(slab, slab, ring2_send.at[step], ring2_recv.at[step], to)

    def pair2_copy(step):
        slab = whole_two.at[:, :, :, :, core, at_step(step)]
        return remote(slab, slab, pair2_send.at[step], pair2_recv.at[step], sibling)

    def pass_on(axis, step):
        many(15, plane2_send.at[step], plane2_recv.at[step]).wait_recv()
        for index in (1, 3, 2):
            ring2_copy(axis, step, index).start()

    def to_other_core(step):
        many(48, ring2_send.at[step], ring2_recv.at[step]).wait_recv()
        pair2_copy(step).start()

    my_group = col * ROWS + row

    @pl.loop(0, BLOCKS)
    def _(step):
        block = plane_of(step)

        pair_copy(step, block).wait_recv()

        @pl.loop(0, 4)
        def _(depth):
            lower = lax.broadcasted_iota(jnp.int32, (CHUNK, 128), 1) < 64
            for part in range(4):
                one = whole_one[block, 0, depth, part // 2, part % 2].astype(F32) * LOG2E
                two = whole_one[block, 1, depth, part // 2, part % 2].astype(F32) * LOG2E
                left = jnp.where(lower, one, pltpu.roll(two, 64, 1))
                right = jnp.where(lower, pltpu.roll(one, 64, 1), two)
                first = depth * 128 + part * 32
                for head in range(H):
                    bias_f[head, pl.ds(first, 16), :] = left[head * 16 : (head + 1) * 16]
                    bias_f[head, pl.ds(first + 16, 16), :] = right[head * 16 : (head + 1) * 16]

        def fetch_next():
            @pl.when(step == 0)
            def _():
                ring_copy(3).wait_recv()
                onward_copy(3).start()
                pair_copy(1, plane_of(1)).start()
                ring_copy(1).wait_recv()
                onward_copy(1).start()
                pair_copy(2, plane_of(2)).start()

            @pl.when(step == 1)
            def _():
                onward_copy(1).wait_recv()
                onward_copy(3).wait_recv()
                pair_copy(3, plane_of(3)).start()

        middle = attend(block, out_one_ref[...], fetch_next).astype(BF16).astype(F32)
        found = dot_nt(bias_two_t, layer_norm(middle, gain_two).astype(BF16))
        for line in range(OWN):
            for head in range(H):
                small_f[head * OWN + line, :] = found[head, line * LANES : (line + 1) * LANES]
        whole_two[x, ylo, z, yhi, core, at_step(step)] = small_f[...].astype(BF16)

        @pl.when(step == 0)
        def _():
            pl.semaphore_wait(joined, 3)

        for parity, axis in enumerate("yz"):
            @pl.when(lax.rem(step, 2) == parity)
            def _():
                for index in FAR_FIRST:
                    plane2_copy(axis, step, index).start()

        line_f[...] = middle
        for line in range(OWN):
            for place in range(OWN):
                flat_f[pl.ds(line * OWN + place, 32, 16), :] = line_f[pl.ds(line * LANES + place, 32, OWN), :]
        tiles[pl.ds(block * 32, 32)] = flat_f[:512].astype(BF16).reshape(32, 16, C)

        @pl.loop(0, 32, unroll=8)
        def _(index):
            group = block * 32 + lax.rem(index + me, 32)

            @pl.when(group != my_group)
            def _():
                tile_copy(group).start()

        for late, axis in ((2, "y"), (3, "z")):
            @pl.when(step == late)
            def _():
                pass_on(axis, late - 2)

    pass_on("y", 2)
    to_other_core(0)
    pass_on("z", 3)
    to_other_core(1)
    columns[me] = tiles[my_group]

    all_tiles().wait_recv()
    flat_f[...] = columns[...].reshape(DEVS * 16, C).astype(F32)

    for line in range(OWN):
        line_parts(line, flat_f[pl.ds(line, N, OWN), :], gain_two, proj_two_ref, proj_two_t)
        if line == 1:
            to_other_core(2)
    to_other_core(3)
    for step in range(BLOCKS):
        pair2_copy(step).wait_recv()

    def back_copy(other):
        return remote(
            result.at[other], landed.at[row], back_send, back_recv, (other, col)
        )

    @pl.loop(0, BLOCKS)
    def _(step):
        block = lax.rem(x + jnp.where(step == 0, 2, jnp.where(step == 2, 3, jnp.where(step == 3, 0, 1))), 4)
        for plane in range(4):
            delta = lax.rem(block - plane + 4, 4)
            made = jnp.where(delta == 2, 3, jnp.where(delta == 3, 2, delta))
            flat_f[plane * 512 : (plane + 1) * 512, :] = (
                whole_two[plane, :, :, :, :, at_step(made)].reshape(512, 128).astype(F32) * LOG2E
            )
        for head in range(H):
            for line in range(OWN):
                bias_f[head, pl.ds(line, DEVS, OWN), :] = flat_f[pl.ds(head * OWN + line, DEVS, 16), :]

        found = attend(block, out_two_ref[...], lambda: None)
        for line in range(OWN):
            flat_f[pl.ds(line, LANES, OWN), :] = found[line * LANES : (line + 1) * LANES]
        result[pl.ds(block * 2, 2)] = flat_f[:512].astype(BF16).reshape(2, 256, C)
        for side in range(2):
            @pl.when(block * 2 + side != row)
            def _():
                back_copy(block * 2 + side).start()

    own_result = pltpu.make_async_copy(result.at[row], landed.at[row], own_sem)
    own_result.start()
    own_result.wait()

    many(60, plane_send, plane_recv).wait_send()
    for step in (1, 3):
        ring_copy(step).wait_send()
        onward_copy(step).wait_send()
    for step in range(BLOCKS):
        pair_copy(step, plane_of(step)).wait_send()
        many(64, pair2_send.at[step], pair2_recv.at[step]).wait_send()
        many(15, plane2_send.at[step], plane2_recv.at[step]).wait_send()
        many(48, ring2_send.at[step], ring2_recv.at[step]).wait_send()
    all_tiles().wait_send()

    all_back = many(7 * 16, back_send, back_recv)
    all_back.wait_recv()
    all_back.wait_send()


def arrange(landed_ref, block_ref, flat_f, block_f):
    for source in range(ROWS):
        flat_f[...] = landed_ref[source].astype(F32)
        for place in range(OWN):
            block_f[pl.ds(source * OWN + place, 16, COLS_HERE), :] = flat_f[pl.ds(place, 16, OWN), :]
    block_ref[...] = block_f[...].astype(BF16).reshape(16, COLS_HERE, C)


def body(pair, gain_one, proj_one, bias_one, out_one, gain_two, proj_two, bias_two, out_two):
    dma = pltpu.SemaphoreType.DMA
    gathered = pltpu.VMEM((4, 2, 4, 2, 2, CHUNK, 128), BF16)
    landed = pl.pallas_call(
        kernel,
        out_shape=jax.ShapeDtypeStruct((ROWS, 256, C), BF16),
        in_specs=[pl.BlockSpec(memory_space=pltpu.HBM)] * 9,
        out_specs=pl.BlockSpec(memory_space=pl.ANY),
        scratch_shapes=[
            pltpu.VMEM((ROWS_HERE, COLS_HERE, C), BF16),
            pltpu.VMEM((1, C), BF16),
            pltpu.VMEM((C, 4 * C), BF16),
            pltpu.VMEM((H, C), BF16),
            pltpu.VMEM((C, C), BF16),
            pltpu.VMEM((1, C), BF16),
            pltpu.VMEM((C, 4 * C), BF16),
            pltpu.VMEM((H, C), BF16),
            pltpu.VMEM((C, C), BF16),
            dma((9,)),
            pltpu.VMEM((COLS, OWN, COLS_HERE, C), BF16),
            gathered,
            gathered,
            pltpu.VMEM((DEVS, 16, C), BF16),
            pltpu.VMEM((DEVS, 16, C), BF16),
            pltpu.VMEM((ROWS, 256, C), BF16),
            pltpu.VMEM((DEVS * 16, C), F32),
            pltpu.VMEM((CHUNK, 128), F32),
            pltpu.VMEM((16, 128), F32),
            pltpu.VMEM((OWN * LANES, C), F32),
            pltpu.VMEM((H, N, LANES), F32),
            pltpu.VMEM((OWN, BLOCKS, LANES, C), F32),
            pltpu.VMEM((OWN, BLOCKS, H * LANES, C), BF16),
            pltpu.VMEM((OWN, N, C), BF16),
            pltpu.VMEM((OWN, C + ONES, N), BF16),
            pltpu.VMEM((OWN, BLOCKS, C, LANES), F32),
            pltpu.VMEM((OWN, N, H * LANES), BF16),
            dma, dma, dma,
            dma, dma, dma((4,)), dma((4,)), dma((4,)), dma((4,)),
            dma, dma,
            dma((BLOCKS,)), dma((BLOCKS,)), dma((BLOCKS,)), dma((BLOCKS,)), dma((BLOCKS,)), dma((BLOCKS,)),
            dma, dma, pltpu.SemaphoreType.REGULAR,
        ],
        compiler_params=pltpu.CompilerParams(
            collective_id=0, has_side_effects=True, vmem_limit_bytes=60 * 1024 * 1024
        ),
        name="triangle",
    )(
        pair, gain_one.reshape(1, C), proj_one, bias_one.T, out_one,
        gain_two.reshape(1, C), proj_two, bias_two.T, out_two,
    )
    return landed.reshape(ROWS, ROWS_HERE, OWN, C).transpose(1, 0, 2, 3).reshape(ROWS_HERE, COLS_HERE, C)


def solution(mesh):
    in_specs = (P("row", "col", None), P(), P(), P(), P(), P(), P(), P(), P())
    out_specs = P("row", "col", None)
    return jax.shard_map(body, mesh=mesh, in_specs=in_specs, out_specs=out_specs, check_vma=False)
```
